256 devices in a mesh: camtime: 16 (over z, x_lo), heads: 16 (over x_hi, y, core).
Axes of the slice: x: 4 (x_hi: 2, x_lo: 2; x = x_hi * 2 + x_lo), y: 4, z: 8, core: 2. Of those that a mesh axis runs over, the one named last changes fastest.
Arguments:
- hidden_patch_vectors: bfloat16 [16, 6, 128, 2048], P('camtime', None, None, 'heads'), may hold values from -6 to 6
- entry_rms_multiplier: float32 [2048], replicated, may hold values from 0.1 to 1.9
- lookup_projection_matrix: bfloat16 [2048, 3, 2048], P(None, None, 'heads')
- exit_projection_matrix: bfloat16 [2048, 2048], P('heads'), may hold values from -0.5 to 0.5
- probe_sharpness: float32 [16], P('heads'), may hold values from 0.5 to 32
- adjacent_camera_pairs: int32 [6, 2], replicated, may hold values from 0 to 5, as said below
- prior_frame_allowed: int32 [16, 6], replicated, may hold values 0 or 1
Outputs:
- attended: bfloat16 [16, 6, 128, 2048], P('camtime', None, None, 'heads')
The draws below stay inside these ranges and needn't reach their ends.
Inputs may be any that keep to these rules, and one draw needn't show every extreme that they name: adjacent_camera_pairs[c, 0] and adjacent_camera_pairs[c, 1] are the cameras before and after camera c on one loop that passes through all 6 cameras once.
All inputs are finite; a program needn't handle non-finite values.
Results may differ from the reference program's by a relative error of at most 0.018.
The reference program's roundings to bfloat16 on the way (of `scaled`, `weights`, `mixed` and `part`) count: a program that leaves them out, or rounds other values in their place, can miss the bound.
Values may be sent and summed in bfloat16 or wider, within the bound.
A program may use at most 64 MiB of HBM per device.

```python
import math
import jax
import jax.numpy as jnp
from jax import lax

D = 2048
PROBE_COUNT = 16
PROBE_DEPTH = 128
CAMS = 6
PATCHES = 128
FRAMES = 16
N_HEADS = 16


def draw_adjacent_camera_pairs(key, part):
    key = jax.random.fold_in(key, 7)
    order = jax.random.permutation(key, CAMS).astype(jnp.int32)
    place = jnp.argsort(order).astype(jnp.int32)
    before = order[(place - 1) % CAMS]
    after = order[(place + 1) % CAMS]
    return jnp.stack([before, after], axis=1).astype(jnp.int32)


def draw_hidden_patch_vectors(key, part):
    key = jax.random.fold_in(key, 11)
    keys = jax.random.split(key, 3)
    row_scale = jnp.exp(jax.random.uniform(keys[0], (FRAMES, CAMS, PATCHES, 1), jnp.float32, -0.7, 0.7))
    values = jax.random.normal(keys[2], (FRAMES, CAMS, PATCHES, D), jnp.float32) * row_scale
    return jnp.clip(values, -6.0, 6.0).astype(jnp.bfloat16)


def draw_lookup_projection_matrix(key, part):
    key = jax.random.fold_in(key, 13)
    keys = jax.random.split(key, 1)
    exponent_divisor = 1.0 / jnp.sqrt(jnp.float32(D))
    weights = jnp.clip(jax.random.normal(keys[0], (D, 3, D), jnp.float32), -6.0, 6.0) * exponent_divisor
    return weights.astype(jnp.bfloat16)


def place_ends(values, own_key, smallest, largest):
    longest = values.shape.index(max(values.shape))
    spots = []
    for shift in (0, 1):
        where = [jax.random.randint(jax.random.fold_in(own_key, axis), (), 0, length) for axis, length in enumerate(values.shape)]
        where[longest] = (where[longest] + shift) % values.shape[longest]
        spots.append(tuple(where))
    return values.at[spots[0]].set(smallest).at[spots[1]].set(largest)


def shard_levels(rng, dims, pieces, smallest, largest):
    def one(dim, shards_of):
        steps = jax.random.uniform(jax.random.fold_in(jax.random.fold_in(rng, 6), dim), (shards_of,), jnp.float32, smallest / len(pieces), largest / len(pieces))
        return jnp.repeat(jnp.exp(steps), dims[dim] // shards_of).reshape((-1,) + (1,) * (len(dims) - dim - 1))

    factor_of = one(*pieces[0])
    for cut in pieces[1:]:
        factor_of = factor_of * one(*cut)
    return factor_of


def gaussian(own_key, extent, deviation, bound, pieces=(), kind=jnp.bfloat16):
    level = shard_levels(own_key, extent, pieces, -0.22, 0.18) if pieces else 1.0
    array = jax.random.normal(own_key, extent, jnp.float32) * deviation * level
    return jnp.minimum(jnp.maximum(array, -bound), bound).astype(kind)


def setup_inputs(seed: int = 0) -> dict:
    seeds = jax.random.split(jax.random.key(seed), 8)
    return {
        "hidden_patch_vectors": draw_hidden_patch_vectors(jax.random.fold_in(seeds[7], 71), 0),
        "entry_rms_multiplier": jnp.clip(1.0 + 0.18 * jax.random.normal(seeds[1], (D,), jnp.float32), 0.1, 1.9),
        "lookup_projection_matrix": draw_lookup_projection_matrix(jax.random.fold_in(seeds[7], 71), 0),
        "exit_projection_matrix": gaussian(seeds[3], (D, D), PROBE_DEPTH ** -0.5, 0.5, ((0, 16),)),
        "probe_sharpness": jnp.clip(jnp.exp(math.log(32.0) - 4.158883 * jax.random.uniform(seeds[4], (PROBE_COUNT,), jnp.float32) ** shard_levels(seeds[4], (PROBE_COUNT,), ((0, 16),), -0.2, 0.2)), 0.5, 32.0),
        "adjacent_camera_pairs": draw_adjacent_camera_pairs(jax.random.fold_in(seeds[7], 71), 0),
        "prior_frame_allowed": place_ends((jax.random.randint(seeds[6], (FRAMES, CAMS), 0, 4) < 3).astype(jnp.int32), jax.random.fold_in(seeds[6], 1), 0, 1),
    }


def unit_rows(raw):
    return (raw * lax.rsqrt(lax.optimization_barrier(jnp.mean(raw * raw, axis=-1, keepdims=True)) + 1e-06)).astype(jnp.bfloat16)

def reference(hidden_patch_vectors, entry_rms_multiplier, lookup_projection_matrix, exit_projection_matrix, probe_sharpness, adjacent_camera_pairs, prior_frame_allowed):
    total_rows = FRAMES * CAMS * PATCHES
    tokens = hidden_patch_vectors.reshape(total_rows, D)
    wide = tokens.astype(jnp.float32)
    scaled = (wide * entry_rms_multiplier[None, :]).astype(jnp.bfloat16)
    inv_rms = lax.rsqrt(lax.optimization_barrier(jnp.mean(wide * wide, axis=1)) + 1e-06)
    raw = jnp.dot(scaled, lookup_projection_matrix.reshape(D, 3 * D), preferred_element_type=jnp.float32) * inv_rms[:, None]
    raw = raw.reshape(FRAMES, CAMS, PATCHES, 3, PROBE_COUNT, PROBE_DEPTH)
    query = unit_rows(raw[:, :, :, 0])
    key = unit_rows(raw[:, :, :, 1])
    value = raw[:, :, :, 2].astype(jnp.bfloat16)
    index_table = jnp.concatenate([jnp.arange(CAMS, dtype=jnp.int32)[:, None], adjacent_camera_pairs.astype(jnp.int32)], axis=1)
    frame_ids = jnp.arange(FRAMES, dtype=jnp.int32)

    def frame_head(frame, probe_number):
        q_now = lax.dynamic_index_in_dim(query, frame, 0, keepdims=False)[:, :, probe_number].astype(jnp.float32)
        k_now = lax.dynamic_index_in_dim(key, frame, 0, keepdims=False)[:, :, probe_number]
        v_now = lax.dynamic_index_in_dim(value, frame, 0, keepdims=False)[:, :, probe_number]
        k_cross = k_now[index_table].reshape(CAMS, 3 * PATCHES, PROBE_DEPTH).astype(jnp.float32)
        v_cross = v_now[index_table].reshape(CAMS, 3 * PATCHES, PROBE_DEPTH).astype(jnp.float32)
        k_time = jnp.transpose(key[:, :, :, probe_number], (1, 0, 2, 3)).reshape(CAMS, FRAMES * PATCHES, PROBE_DEPTH).astype(jnp.float32)
        v_time = jnp.transpose(value[:, :, :, probe_number], (1, 0, 2, 3)).reshape(CAMS, FRAMES * PATCHES, PROBE_DEPTH).astype(jnp.float32)
        valid = (frame_ids[:, None] < frame) & (prior_frame_allowed == 1)
        valid = jnp.repeat(jnp.transpose(valid), PATCHES, axis=1)
        exponent_divisor = probe_sharpness[probe_number] / jnp.sqrt(jnp.float32(PROBE_DEPTH))
        s_cross = jnp.einsum('cpe,cke->cpk', q_now, k_cross) * exponent_divisor
        s_time = jnp.einsum('cpe,cke->cpk', q_now, k_time) * exponent_divisor
        s_time = jnp.where(valid[:, None, :], s_time, -jnp.inf)
        score = jnp.concatenate([s_cross, s_time], axis=2)
        top = lax.optimization_barrier(jnp.max(score, axis=2, keepdims=True))
        expo = jnp.exp(score - top)
        total = lax.optimization_barrier(jnp.sum(expo, axis=2))
        weights = expo.astype(jnp.bfloat16).astype(jnp.float32)
        values_all = jnp.concatenate([v_cross, v_time], axis=1)
        mixed = jnp.einsum('cpk,cke->cpe', weights, values_all) / total[:, :, None]
        return mixed.astype(jnp.bfloat16)

    def one_frame(frame):
        return lax.map(lambda probe_number: frame_head(frame, probe_number), jnp.arange(PROBE_COUNT, dtype=jnp.int32))
    mixed = lax.map(one_frame, frame_ids)
    mixed = jnp.transpose(mixed, (0, 2, 3, 1, 4)).reshape(total_rows, D)
    group = D // N_HEADS
    summed = jnp.zeros((total_rows, D), jnp.float32)
    for index in range(N_HEADS):
        part = jnp.dot(mixed[:, index * group:(index + 1) * group], exit_projection_matrix[index * group:(index + 1) * group], preferred_element_type=jnp.float32)
        summed = summed + lax.optimization_barrier(part.astype(jnp.bfloat16)).astype(jnp.float32)
    return summed.astype(jnp.bfloat16).reshape(FRAMES, CAMS, PATCHES, D)
```

```python
import functools

import jax
import jax.numpy as jnp
from jax import lax
from jax.experimental import pallas as pl
from jax.experimental.pallas import tpu as pltpu
from jax.sharding import PartitionSpec as P

HEADS = 16
PLANES = 8
GROUP = 3
DEPTH = 128
PATCH = 128
WIDTH = HEADS * DEPTH
ROWS = 2 * PATCH
MASKED = -3e38
LOWEST = -1e30
LOG2E = 1.4426950408889634
UP = (4, 4, 3)
DOWN = (3, 3, 4)
AG_SENDS = 15


def unit_rows(raw):
    return raw * lax.rsqrt(jnp.mean(raw * raw, axis=-1, keepdims=True) + 1e-06)


def kernel(
    x_ref, gain_ref, w_hbm, e_hbm, sharp_ref, adj_ref, allowed_ref, out_ref,
    xg, mg, kv, kc, w_ref, e_ref, e_all, scaled, qt, top_ref, total_ref, acc_ref, ostage, oland,
    x_recv, x_send, m_recv, m_send, a_recv, a_send, up_recv, up_send, dn_recv, dn_send,
    c_recv, c_send, e_recv, e_send, o_recv, o_send, load_sem,
):
    t = lax.axis_index("camtime")
    h = lax.axis_index("heads")
    z, j = t // 2, t % 2
    a, y, p = h // 8, (h // 2) % 4, h % 2

    def head(a_, y_, p_):
        return a_ * 8 + y_ * 2 + p_

    y_up, y_dn, y_far = (y + 1) % 4, (y + 3) % 4, (y + 2) % 4
    h_x, h_up, h_dn, h_sib = head(1 - a, y, p), head(a, y_up, p), head(a, y_dn, p), head(a, y, 1 - p)
    t_x = z * 2 + 1 - j
    t_up = ((z + 1) % PLANES) * 2 + j
    t_dn = ((z + PLANES - 1) % PLANES) * 2 + j
    mine = GROUP * j
    theirs = GROUP * (1 - j)

    def remote(src, dst, send, recv, heads=None, camtime=None):
        return pltpu.make_async_remote_copy(
            src_ref=src, dst_ref=dst, send_sem=send, recv_sem=recv,
            device_id={"camtime": t if camtime is None else camtime, "heads": h if heads is None else heads},
            device_id_type=pl.DeviceIdType.MESH,
        )

    def arrived(ref, sem):
        pltpu.make_async_copy(ref, ref, sem).wait()

    barrier = pltpu.get_barrier_semaphore()

    def greet(camtime, heads):
        pl.semaphore_signal(
            barrier, inc=1, device_id={"camtime": camtime, "heads": heads}, device_id_type=pl.DeviceIdType.MESH
        )

    for other in range(1, HEADS):
        greet(t, (h + other) % HEADS)
    greet(t_x, h)
    greet(t_up, h)
    greet(t_dn, h)

    w_load = pltpu.make_async_copy(w_hbm, w_ref, load_sem.at[0])
    w_load.start()
    e_load = pltpu.make_async_copy(e_hbm, e_ref, load_sem.at[1])
    e_load.start()
    for c in range(GROUP):
        xg[c, h, j] = x_ref[mine + c]
        top_ref[c] = jnp.full((1, ROWS), LOWEST, jnp.float32)
        total_ref[c] = jnp.zeros((1, ROWS), jnp.float32)
        acc_ref[c] = jnp.zeros((DEPTH, ROWS), jnp.float32)
    pl.semaphore_wait(barrier, HEADS + 2)

    swaps = []
    for c in range(GROUP):
        copy = remote(x_ref.at[theirs + c], xg.at[c, h, j], a_send.at[c], a_recv.at[c], camtime=t_x)
        copy.start()
        swaps.append(copy)

    class Gather:
        def __init__(self, buf, recv, send):
            self.buf, self.recv, self.send, self.sent = buf, recv, send, [[] for _ in range(GROUP)]

        def push(self, c, slot, to):
            copy = remote(
                self.buf.at[c, slot], self.buf.at[c, slot], self.send.at[c, len(self.sent[c])],
                self.recv.at[c, slot], heads=to,
            )
            copy.start()
            self.sent[c].append(copy)

        def take(self, c, slot):
            arrived(self.buf.at[c, slot], self.recv.at[c, slot])

        def own(self, c):
            for to in (h_x, h_up, h_dn, h_sib):
                self.push(c, h, to)

        def across(self, c):
            self.take(c, h_x)
            for to in (h_up, h_dn, h_sib):
                self.push(c, h_x, to)

        def near(self, c):
            slot = head(a, y_dn, p)
            self.take(c, slot)
            self.push(c, slot, h_up)
            self.push(c, slot, h_sib)
            slot = head(a, y_up, p)
            self.take(c, slot)
            self.push(c, slot, h_sib)
            slot = head(1 - a, y_up, p)
            self.take(c, slot)
            self.push(c, slot, h_dn)
            self.push(c, slot, h_sib)
            slot = head(1 - a, y_dn, p)
            self.take(c, slot)
            self.push(c, slot, h_sib)

        def far(self, c):
            for a_ in (a, 1 - a):
                slot = head(a_, y_far, p)
                self.take(c, slot)
                self.push(c, slot, h_sib)

        def rest(self, c):
            for a_ in range(2):
                for y_ in range(4):
                    self.take(c, head(a_, y_, 1 - p))

    xs = Gather(xg, x_recv, x_send)
    ms = Gather(mg, m_recv, m_send)

    scale = sharp_ref[0] * (LOG2E / DEPTH**0.5)

    def up_copy(c, d):
        src = kc.at[mine + c] if d == 0 else kv.at[z - d, c]
        return remote(src, kv.at[z - d, c], up_send.at[c, d], up_recv.at[c, d], camtime=t_up)

    def dn_copy(c, hop):
        plane = (z + hop) % PLANES
        src = kc.at[mine + c] if hop == 0 else kv.at[plane, c]
        return remote(src, kv.at[plane, c], dn_send.at[c, hop], dn_recv.at[c, hop], camtime=t_dn)

    def cross_copy(c):
        return remote(kc.at[mine + c], kc.at[mine + c], c_send.at[c], c_recv.at[c], camtime=t_x)

    def project(c):
        squares = jnp.zeros((ROWS, DEPTH), jnp.float32)
        for d in range(HEADS):
            wide = xg[c, d].reshape(ROWS, DEPTH).astype(jnp.float32)
            squares = squares + wide * wide
            scaled[:, d * DEPTH:(d + 1) * DEPTH] = (wide * gain_ref[d:d + 1, :]).astype(jnp.bfloat16)
        inv_rms = lax.rsqrt(jnp.sum(squares, axis=1, keepdims=True) / WIDTH + 1e-06)
        raw = jnp.dot(scaled[...], w_ref[...], preferred_element_type=jnp.float32) * inv_rms
        query = unit_rows(raw[:, :DEPTH])
        key = unit_rows(raw[:, DEPTH:2 * DEPTH]).astype(jnp.bfloat16)
        value = raw[:, 2 * DEPTH:]
        qt[c] = query.T.astype(jnp.bfloat16)
        for f in range(2):
            kc[mine + c, f] = key[f * PATCH:(f + 1) * PATCH]
            kc[mine + c, 2 + f] = value[f * PATCH:(f + 1) * PATCH].T.astype(jnp.bfloat16)

        @pl.when(z < PLANES - 1)
        def _():
            up_copy(c, 0).start()

        @pl.when(z < DOWN[c])
        def _():
            dn_copy(c, 0).start()

        cross_copy(c).start()

    def bias(plane, f, c):
        return jnp.where(allowed_ref[2 * plane + f, mine + c] == 1, 0.0, MASKED).astype(jnp.float32)

    def fold(c, score, values, lanes):
        before = top_ref[c, :, lanes]
        top = jnp.maximum(before, jnp.max(score, axis=0, keepdims=True))
        expo = jnp.exp2(score - top)
        rescale = jnp.exp2(before - top)
        top_ref[c, :, lanes] = top
        total_ref[c, :, lanes] = total_ref[c, :, lanes] * rescale + jnp.sum(expo, axis=0, keepdims=True)
        acc_ref[c, :, lanes] = acc_ref[c, :, lanes] * rescale + jnp.dot(
            values, expo.astype(jnp.bfloat16), preferred_element_type=jnp.float32
        )

    def attend(c, plane):
        score = jnp.dot(kv[plane, c, 0:2].reshape(ROWS, DEPTH), qt[c], preferred_element_type=jnp.float32) * scale
        score = jnp.concatenate(
            [score[:PATCH] + bias(plane, 0, c), score[PATCH:] + bias(plane, 1, c)], axis=0
        )
        values = jnp.concatenate([kv[plane, c, 2], kv[plane, c, 3]], axis=1)
        fold(c, score, values, slice(0, ROWS))

    def attend_cross(c):
        cam = mine + c
        for f in range(2):
            lanes = slice(f * PATCH, (f + 1) * PATCH)
            near = [cam, adj_ref[cam, 0], adj_ref[cam, 1]]
            keys = [kc[n, f] for n in near]
            values = [kc[n, 2 + f] for n in near]
            if f == 1:
                keys.append(kc[cam, 0])
                values.append(kc[cam, 2])
            score = jnp.dot(jnp.concatenate(keys, axis=0), qt[c, :, lanes], preferred_element_type=jnp.float32) * scale
            if f == 1:
                score = jnp.concatenate([score[:3 * PATCH], score[3 * PATCH:] + bias(z, 0, c)], axis=0)
            fold(c, score, jnp.concatenate(values, axis=1), lanes)

    def step_up(c, d):
        @pl.when(z >= d)
        def _():
            arrived(kv.at[z - d, c], up_recv.at[c, d - 1])
            if d < UP[c]:
                @pl.when(z < PLANES - 1)
                def _():
                    up_copy(c, d).start()
            attend(c, z - d)

    def step_dn(c, hop):
        plane = (z + hop) % PLANES

        @pl.when(plane < DOWN[c])
        def _():
            arrived(kv.at[plane, c], dn_recv.at[c, hop - 1])
            if hop < DOWN[c]:
                dn_copy(c, hop).start()

            @pl.when(plane < z)
            def _():
                attend(c, plane)

    def finish(c):
        mixed = acc_ref[c] / total_ref[c]
        mg[c, h] = mixed.T.astype(jnp.bfloat16).reshape(2, PATCH, DEPTH)
        ms.own(c)

    def out_copy(c):
        return remote(ostage.at[c, 1 - j], oland.at[c], o_send.at[c], o_recv.at[c], camtime=t_x)

    def project_out(c):
        summed = jnp.zeros((ROWS, DEPTH), jnp.float32)
        for d in range(HEADS):
            part = jnp.dot(mg[c, d].reshape(ROWS, DEPTH), e_all[d], preferred_element_type=jnp.float32)
            summed = summed + part.astype(jnp.bfloat16).astype(jnp.float32)
        ostage[c] = summed.astype(jnp.bfloat16).reshape(2, PATCH, DEPTH)
        out_copy(c).start()
        out_ref[mine + c] = ostage[c, j]

    for c in range(GROUP):
        arrived(xg.at[c, h, 1 - j], a_recv.at[c])
        xs.own(c)
    for c in range(GROUP):
        xs.across(c)
    w_load.wait()

    xs.near(0)
    xs.far(0)
    xs.rest(0)
    project(0)
    xs.near(1)
    xs.far(1)
    xs.rest(1)
    project(1)
    step_up(0, 1)
    step_dn(0, 1)
    xs.near(2)
    xs.far(2)
    xs.rest(2)
    project(2)

    e_load.wait()
    e_sends = []
    for other in range(1, HEADS):
        to = (h + other) % HEADS
        copy = remote(
            e_ref.at[:, pl.ds(pl.multiple_of(to * DEPTH, DEPTH), DEPTH)], e_all.at[h],
            e_send.at[other], e_recv.at[h], heads=to,
        )
        copy.start()
        e_sends.append(copy)
    e_all[h] = e_ref[:, pl.ds(pl.multiple_of(h * DEPTH, DEPTH), DEPTH)]

    step_up(1, 1)
    step_dn(1, 1)
    step_up(0, 2)
    step_dn(0, 2)
    step_up(2, 1)
    step_dn(2, 1)
    step_up(0, 3)
    step_dn(0, 3)
    step_up(1, 2)
    step_dn(1, 2)
    for c in range(GROUP):
        arrived(kc.at[theirs + c], c_recv.at[c])
    attend_cross(0)
    step_up(0, 4)
    finish(0)
    step_up(1, 3)
    step_dn(1, 3)
    step_up(2, 2)
    step_dn(2, 2)
    ms.across(0)
    attend_cross(1)
    step_up(1, 4)
    finish(1)
    ms.near(0)
    ms.across(1)
    step_up(2, 3)
    step_dn(2, 3)
    attend_cross(2)
    step_dn(2, 4)
    finish(2)
    ms.far(0)
    ms.near(1)
    ms.across(2)
    ms.rest(0)
    for other in range(1, HEADS):
        slot = (h + other) % HEADS
        arrived(e_all.at[slot], e_recv.at[slot])
    project_out(0)
    ms.far(1)
    ms.near(2)
    ms.rest(1)
    project_out(1)
    ms.far(2)
    ms.rest(2)
    project_out(2)
    for c in range(GROUP):
        arrived(oland.at[c], o_recv.at[c])
        out_ref[theirs + c] = oland[c]

    for copy in swaps + e_sends:
        copy.wait_send()
    for c in range(GROUP):
        for copy in xs.sent[c] + ms.sent[c]:
            copy.wait_send()
        cross_copy(c).wait_send()
        out_copy(c).wait_send()
        for d in range(UP[c]):
            @pl.when((z >= d) & (z < PLANES - 1))
            def _():
                up_copy(c, d).wait_send()
        for hop in range(DOWN[c]):
            @pl.when((z + hop) % PLANES < DOWN[c])
            def _():
                dn_copy(c, hop).wait_send()


def on_device(
    hidden_patch_vectors,
    entry_rms_multiplier,
    lookup_projection_matrix,
    exit_projection_matrix,
    probe_sharpness,
    adjacent_camera_pairs,
    prior_frame_allowed,
):
    frames, cams, patches, local_width = hidden_patch_vectors.shape
    vmem = pl.BlockSpec(memory_space=pltpu.VMEM)
    smem = pl.BlockSpec(memory_space=pltpu.SMEM)
    hbm = pl.BlockSpec(memory_space=pl.ANY)
    dma = pltpu.SemaphoreType.DMA
    bf16, f32 = jnp.bfloat16, jnp.float32
    result = pl.pallas_call(
        kernel,
        out_shape=jax.ShapeDtypeStruct((cams, patches, local_width), bf16),
        in_specs=[vmem, vmem, hbm, hbm, smem, smem, smem],
        out_specs=vmem,
        scratch_shapes=[
            pltpu.VMEM((GROUP, HEADS, 2, PATCH, DEPTH), bf16),
            pltpu.VMEM((GROUP, HEADS, 2, PATCH, DEPTH), bf16),
            pltpu.VMEM((PLANES, GROUP, 4, PATCH, DEPTH), bf16),
            pltpu.VMEM((2 * GROUP, 4, PATCH, DEPTH), bf16),
            pltpu.VMEM((WIDTH, 3 * DEPTH), bf16),
            pltpu.VMEM((DEPTH, WIDTH), bf16),
            pltpu.VMEM((HEADS, DEPTH, DEPTH), bf16),
            pltpu.VMEM((ROWS, WIDTH), bf16),
            pltpu.VMEM((GROUP, DEPTH, ROWS), bf16),
            pltpu.VMEM((GROUP, 1, ROWS), f32),
            pltpu.VMEM((GROUP, 1, ROWS), f32),
            pltpu.VMEM((GROUP, DEPTH, ROWS), f32),
            pltpu.VMEM((GROUP, 2, PATCH, DEPTH), bf16),
            pltpu.VMEM((GROUP, PATCH, DEPTH), bf16),
            dma((GROUP, HEADS)), dma((GROUP, AG_SENDS)),
            dma((GROUP, HEADS)), dma((GROUP, AG_SENDS)),
            dma((GROUP,)), dma((GROUP,)),
            dma((GROUP, 4)), dma((GROUP, 4)),
            dma((GROUP, 4)), dma((GROUP, 4)),
            dma((GROUP,)), dma((GROUP,)),
            dma((HEADS,)), dma((HEADS,)),
            dma((GROUP,)), dma((GROUP,)),
            dma((2,)),
        ],
        compiler_params=pltpu.CompilerParams(
            collective_id=0, has_side_effects=True, vmem_limit_bytes=48 * 1024 * 1024
        ),
    )(
        hidden_patch_vectors.reshape(cams, patches, local_width),
        entry_rms_multiplier.reshape(HEADS, DEPTH),
        lookup_projection_matrix.reshape(WIDTH, 3 * DEPTH),
        exit_projection_matrix,
        probe_sharpness,
        adjacent_camera_pairs,
        prior_frame_allowed,
    )
    return result.reshape(frames, cams, patches, local_width)


def solution(mesh):
    placed = (
        P("camtime", None, None, "heads"),
        P(),
        P(None, None, "heads"),
        P("heads", None),
        P("heads"),
        P(),
        P(),
    )
    return jax.shard_map(
        on_device,
        mesh=mesh,
        in_specs=placed,
        out_specs=P("camtime", None, None, "heads"),
        check_vma=False,
    )
```

```python
import jax
import jax.numpy as jnp
from jax import lax
from jax.experimental import pallas as pl
from jax.experimental.pallas import tpu as pltpu
from jax.sharding import PartitionSpec as P

HEADS = 16
ROW = 4
PLANES = 8
GROUP = 3
DEPTH = 128
PATCH = 128
WIDTH = HEADS * DEPTH
ROWS = 2 * PATCH
MASKED = -3e38
LOWEST = -1e30
LOG2E = 1.4426950408889634
UP = (4, 4, 3)
DOWN = (3, 3, 4)


def unit_rows(raw):
    return raw * lax.rsqrt(jnp.mean(raw * raw, axis=-1, keepdims=True) + 1e-06)


def kernel(
    x_hbm, gain_ref, w_hbm, e_hbm, sharp_ref, adj_ref, allowed_ref, out_ref,
    xg, mg, mstage, kv, kc, w_ref, e_ref, e_all, scaled, raw_ref, qt, top_ref, total_ref, acc_ref,
    x_recv, x_sib, x_send, x_sib_send, m_recv, m_sib, m_send, m_sib_send,
    up_recv, up_send, dn_recv, dn_send, c_recv, c_send, e_recv, e_send, load_sem,
):
    t = lax.axis_index("camtime")
    h = lax.axis_index("heads")
    z, j = t // 2, t % 2
    a, y, p = h // 8, (h // 2) % ROW, h % 2

    def head(a_, y_, p_):
        return a_ * 8 + y_ * 2 + p_

    rows = [y, (y + 1) % ROW, (y + 3) % ROW, (y + 2) % ROW]
    h_sib = head(a, y, 1 - p)
    t_x = z * 2 + 1 - j
    t_up = ((z + 1) % PLANES) * 2 + j
    t_dn = ((z + PLANES - 1) % PLANES) * 2 + j
    mine = GROUP * j
    theirs = GROUP * (1 - j)

    def remote(src, dst, send, recv, heads=None, camtime=None):
        return pltpu.make_async_remote_copy(
            src_ref=src, dst_ref=dst, send_sem=send, recv_sem=recv,
            device_id={"camtime": t if camtime is None else camtime, "heads": h if heads is None else heads},
            device_id_type=pl.DeviceIdType.MESH,
        )

    def arrived(ref, sem):
        pltpu.make_async_copy(ref, ref, sem).wait()

    barrier = pltpu.get_barrier_semaphore()

    def greet(camtime, heads):
        pl.semaphore_signal(
            barrier, inc=1, device_id={"camtime": camtime, "heads": heads}, device_id_type=pl.DeviceIdType.MESH
        )

    for other in range(1, HEADS):
        greet(t, (h + other) % HEADS)
    for other in range(0, HEADS, 2):
        greet(t_x, (h + other) % HEADS)
    greet(t_up, h)
    greet(t_dn, h)

    def x_slot(c, p_, y_, a_, f):
        return ((c * 2 + p_) * ROW + y_) * 4 + a_ * 2 + f

    def m_slot(cam, p_, y_, a_):
        return ((cam * 2 + p_) * ROW + y_) * 2 + a_

    for c in range(GROUP):
        pltpu.make_async_copy(x_hbm.at[mine + c], xg.at[x_slot(c, p, y, a, j)], x_recv.at[c, y]).start()
    w_loads = []
    for i in range(3):
        load = pltpu.make_async_copy(w_hbm.at[i], w_ref.at[:, i * DEPTH:(i + 1) * DEPTH], load_sem.at[i])
        load.start()
        w_loads.append(load)
    e_load = pltpu.make_async_copy(e_hbm, e_ref, load_sem.at[3])
    e_load.start()
    for c in range(GROUP):
        top_ref[c] = jnp.full((1, ROWS), LOWEST, jnp.float32)
        total_ref[c] = jnp.zeros((1, ROWS), jnp.float32)
        acc_ref[c] = jnp.zeros((DEPTH, ROWS), jnp.float32)
    pl.semaphore_wait(barrier, HEADS - 1 + HEADS // 2 + 2)

    chips = [(a_, y_) for y_ in rows for a_ in (1 - a, a)]

    def x_push(c):
        slot = x_slot(c, p, y, a, j)
        for n, (a_, y_) in enumerate(chips):
            remote(x_hbm.at[theirs + c], xg.at[slot], x_send.at[c], x_recv.at[c, y],
                   heads=head(a_, y_, p), camtime=t_x).start()
            if n != 1:
                remote(x_hbm.at[mine + c], xg.at[slot], x_send.at[c], x_recv.at[c, y],
                       heads=head(a_, y_, p)).start()

    def x_relay(c):
        for y_ in rows:
            row = xg.at[pl.ds(x_slot(c, p, y_, 0, 0), 4)]
            arrived(row, x_recv.at[c, y_])
            remote(row, row, x_sib_send.at[c], x_sib.at[c, y_], heads=h_sib).start()

    def x_sent(c):
        arrived(xg.at[pl.ds(0, 15)], x_send.at[c])
        arrived(xg.at[pl.ds(0, 16)], x_sib_send.at[c])

    scale = sharp_ref[0] * (LOG2E / DEPTH**0.5)

    def up_copy(c, d):
        src = kc.at[mine + c] if d == 0 else kv.at[z - d, c]
        return remote(src, kv.at[z - d, c], up_send.at[c, d], up_recv.at[c, d], camtime=t_up)

    def dn_copy(c, hop):
        plane = (z + hop) % PLANES
        src = kc.at[mine + c] if hop == 0 else kv.at[plane, c]
        return remote(src, kv.at[plane, c], dn_send.at[c, hop], dn_recv.at[c, hop], camtime=t_dn)

    def cross_copy(c):
        return remote(kc.at[mine + c], kc.at[mine + c], c_send.at[c], c_recv.at[c], camtime=t_x)

    def project(c):
        squares = jnp.zeros((ROWS, DEPTH), jnp.float32)
        for n, y_ in enumerate(rows):
            arrived(xg.at[pl.ds(x_slot(c, 1 - p, y_, 0, 0), 4)], x_sib.at[c, y_])
            for a_ in range(2):
                for p_ in range(2):
                    wide = xg[pl.ds(x_slot(c, p_, y_, a_, 0), 2)].reshape(ROWS, DEPTH).astype(jnp.float32)
                    squares = squares + wide * wide
                    scaled[:, (a_ * 2 + p_) * DEPTH:(a_ * 2 + p_ + 1) * DEPTH] = (
                        wide * gain_ref[head(a_, y_, p_)]
                    ).astype(jnp.bfloat16)
            part = jnp.zeros((ROWS, 3 * DEPTH), jnp.float32) if n == 0 else raw_ref[...]
            for a_ in range(2):
                part = part + jnp.dot(
                    scaled[:, a_ * 2 * DEPTH:(a_ + 1) * 2 * DEPTH],
                    w_ref[pl.ds(pl.multiple_of(head(a_, y_, 0) * DEPTH, 2 * DEPTH), 2 * DEPTH), :],
                    preferred_element_type=jnp.float32,
                )
            raw_ref[...] = part
        inv_rms = lax.rsqrt(jnp.sum(squares, axis=1, keepdims=True) / WIDTH + 1e-06)
        raw = raw_ref[...] * inv_rms
        key = unit_rows(raw[:, DEPTH:2 * DEPTH]).astype(jnp.bfloat16)
        value = raw[:, 2 * DEPTH:]
        for f in range(2):
            kc[mine + c, f] = key[f * PATCH:(f + 1) * PATCH]
            kc[mine + c, 2 + f] = value[f * PATCH:(f + 1) * PATCH].T.astype(jnp.bfloat16)

        @pl.when(z < PLANES - 1)
        def _():
            up_copy(c, 0).start()

        @pl.when(z < DOWN[c])
        def _():
            dn_copy(c, 0).start()

        cross_copy(c).start()
        qt[c] = unit_rows(raw[:, :DEPTH]).T.astype(jnp.bfloat16)

    def bias(plane, f, c):
        return jnp.where(allowed_ref[mine + c, 2 * plane + f] == 1, 0.0, MASKED).astype(jnp.float32)

    def fold(c, score, values, lanes):
        before = top_ref[c, :, lanes]
        top = jnp.maximum(before, jnp.max(score, axis=0, keepdims=True))
        expo = jnp.exp2(score - top)
        rescale = jnp.exp2(before - top)
        top_ref[c, :, lanes] = top
        total_ref[c, :, lanes] = total_ref[c, :, lanes] * rescale + jnp.sum(expo, axis=0, keepdims=True)
        acc_ref[c, :, lanes] = acc_ref[c, :, lanes] * rescale + jnp.dot(
            values, expo.astype(jnp.bfloat16), preferred_element_type=jnp.float32
        )

    def attend(c, plane):
        score = jnp.dot(kv[plane, c, 0:2].reshape(ROWS, DEPTH), qt[c], preferred_element_type=jnp.float32) * scale
        score = jnp.concatenate(
            [score[:PATCH] + bias(plane, 0, c), score[PATCH:] + bias(plane, 1, c)], axis=0
        )
        values = jnp.concatenate([kv[plane, c, 2], kv[plane, c, 3]], axis=1)
        fold(c, score, values, slice(0, ROWS))

    def attend_cross(c):
        if c == 0:
            for other in range(GROUP):
                arrived(kc.at[theirs + other], c_recv.at[other])
        cam = mine + c
        for f in range(2):
            lanes = slice(f * PATCH, (f + 1) * PATCH)
            near = [cam, adj_ref[0, cam], adj_ref[1, cam]]
            keys = [kc[n, f] for n in near]
            values = [kc[n, 2 + f] for n in near]
            if f == 1:
                keys.append(kc[cam, 0])
                values.append(kc[cam, 2])
            score = jnp.dot(jnp.concatenate(keys, axis=0), qt[c, :, lanes], preferred_element_type=jnp.float32) * scale
            if f == 1:
                score = jnp.concatenate([score[:3 * PATCH], score[3 * PATCH:] + bias(z, 0, c)], axis=0)
            fold(c, score, jnp.concatenate(values, axis=1), lanes)

    def step_up(c, d):
        @pl.when(z >= d)
        def _():
            arrived(kv.at[z - d, c], up_recv.at[c, d - 1])
            if d < UP[c]:
                @pl.when(z < PLANES - 1)
                def _():
                    up_copy(c, d).start()
            attend(c, z - d)

    def step_dn(c, hop):
        plane = (z + hop) % PLANES

        @pl.when(plane < DOWN[c])
        def _():
            arrived(kv.at[plane, c], dn_recv.at[c, hop - 1])
            if hop < DOWN[c]:
                dn_copy(c, hop).start()

            @pl.when(plane < z)
            def _():
                attend(c, plane)

    def m_push(c):
        mixed = (acc_ref[c] / total_ref[c]).T.astype(jnp.bfloat16).reshape(2, PATCH, DEPTH)
        mstage[c] = mixed
        cam = mine + c
        slot = m_slot(cam, p, y, a)
        for n, (a_, y_) in enumerate(chips):
            remote(mstage.at[c, 1 - j], mg.at[slot], m_send.at[c], m_recv.at[cam, y],
                   heads=head(a_, y_, p), camtime=t_x).start()
            if n != 1:
                remote(mstage.at[c, j], mg.at[slot], m_send.at[c], m_recv.at[cam, y],
                       heads=head(a_, y_, p)).start()
        mg[slot] = mstage[c, j]

    def m_relay(c):
        for n, y_ in enumerate(rows):
            for side, cam in enumerate((mine + c, theirs + c)):
                row = mg.at[pl.ds(m_slot(cam, p, y_, 0), 2)]
                if n == 0 and side == 0:
                    arrived(mg.at[pl.ds(m_slot(cam, p, y_, 0), 1)], m_recv.at[cam, y_])
                else:
                    arrived(row, m_recv.at[cam, y_])
                remote(row, row, m_sib_send.at[c], m_sib.at[cam, y_], heads=h_sib).start()

    def m_sent(c):
        arrived(xg.at[pl.ds(0, 15)], m_send.at[c])
        arrived(xg.at[pl.ds(0, 16)], m_sib_send.at[c])

    def project_out(c):
        summed = jnp.zeros((ROWS, DEPTH), jnp.float32)
        cams = (mine + c, theirs + c)
        for y_ in rows:
            for cam in cams:
                arrived(mg.at[pl.ds(m_slot(cam, 1 - p, y_, 0), 2)], m_sib.at[cam, y_])
            for a_ in range(2):
                for p_ in range(2):
                    mixed = jnp.concatenate([mg[m_slot(cam, p_, y_, a_)] for cam in cams], axis=0)
                    part = jnp.dot(mixed, e_all[head(a_, y_, p_)], preferred_element_type=jnp.float32)
                    summed = summed + part.astype(jnp.bfloat16).astype(jnp.float32)
        for n, cam in enumerate(cams):
            out_ref[cam] = summed[n * PATCH:(n + 1) * PATCH].astype(jnp.bfloat16)

    for c in range(GROUP):
        x_push(c)
    x_relay(0)
    for load in w_loads:
        load.wait()
    project(0)
    x_relay(1)
    step_up(0, 1)
    step_dn(0, 1)
    project(1)
    x_relay(2)
    step_up(0, 2)
    step_dn(0, 2)
    project(2)

    e_load.wait()
    e_sends = []
    for other in range(1, HEADS):
        to = (h + other) % HEADS
        copy = remote(
            e_ref.at[:, pl.ds(pl.multiple_of(to * DEPTH, DEPTH), DEPTH)], e_all.at[h],
            e_send.at[other], e_recv.at[h], heads=to,
        )
        copy.start()
        e_sends.append(copy)
    e_all[h] = e_ref[:, pl.ds(pl.multiple_of(h * DEPTH, DEPTH), DEPTH)]

    step_up(1, 1)
    step_dn(1, 1)
    step_up(0, 3)
    step_dn(0, 3)
    step_up(1, 2)
    step_dn(1, 2)
    step_up(2, 1)
    step_dn(2, 1)
    attend_cross(0)
    step_up(0, 4)
    m_push(0)
    attend_cross(1)
    step_up(1, 3)
    step_dn(1, 3)
    step_up(2, 2)
    step_dn(2, 2)
    step_up(1, 4)
    m_push(1)
    attend_cross(2)
    m_relay(0)
    step_up(2, 3)
    step_dn(2, 3)
    step_dn(2, 4)
    m_push(2)
    for other in range(1, HEADS):
        slot = (h + other) % HEADS
        arrived(e_all.at[slot], e_recv.at[slot])
    project_out(0)
    m_relay(1)
    project_out(1)
    m_relay(2)
    project_out(2)

    for copy in e_sends:
        copy.wait_send()
    for c in range(GROUP):
        x_sent(c)
        m_sent(c)
        cross_copy(c).wait_send()
        for d in range(UP[c]):
            @pl.when((z >= d) & (z < PLANES - 1))
            def _():
                up_copy(c, d).wait_send()
        for hop in range(DOWN[c]):
            @pl.when((z + hop) % PLANES < DOWN[c])
            def _():
                dn_copy(c, hop).wait_send()


def on_device(
    hidden_patch_vectors,
    entry_rms_multiplier,
    lookup_projection_matrix,
    exit_projection_matrix,
    probe_sharpness,
    adjacent_camera_pairs,
    prior_frame_allowed,
):
    frames, cams, patches, local_width = hidden_patch_vectors.shape
    vmem = pl.BlockSpec(memory_space=pltpu.VMEM)
    smem = pl.BlockSpec(memory_space=pltpu.SMEM)
    hbm = pl.BlockSpec(memory_space=pl.ANY)
    dma = pltpu.SemaphoreType.DMA
    bf16, f32 = jnp.bfloat16, jnp.float32
    result = pl.pallas_call(
        kernel,
        out_shape=jax.ShapeDtypeStruct((cams, patches, local_width), bf16),
        in_specs=[hbm, vmem, hbm, hbm, smem, smem, smem],
        out_specs=vmem,
        scratch_shapes=[
            pltpu.VMEM((GROUP * HEADS * 2, PATCH, DEPTH), bf16),
            pltpu.VMEM((2 * GROUP * HEADS, PATCH, DEPTH), bf16),
            pltpu.VMEM((GROUP, 2, PATCH, DEPTH), bf16),
            pltpu.VMEM((PLANES, GROUP, 4, PATCH, DEPTH), bf16),
            pltpu.VMEM((2 * GROUP, 4, PATCH, DEPTH), bf16),
            pltpu.VMEM((WIDTH, 3 * DEPTH), bf16),
            pltpu.VMEM((DEPTH, WIDTH), bf16),
            pltpu.VMEM((HEADS, DEPTH, DEPTH), bf16),
            pltpu.VMEM((ROWS, 4 * DEPTH), bf16),
            pltpu.VMEM((ROWS, 3 * DEPTH), f32),
            pltpu.VMEM((GROUP, DEPTH, ROWS), bf16),
            pltpu.VMEM((GROUP, 1, ROWS), f32),
            pltpu.VMEM((GROUP, 1, ROWS), f32),
            pltpu.VMEM((GROUP, DEPTH, ROWS), f32),
            dma((GROUP, ROW)), dma((GROUP, ROW)), dma((GROUP,)), dma((GROUP,)),
            dma((2 * GROUP, ROW)), dma((2 * GROUP, ROW)), dma((GROUP,)), dma((GROUP,)),
            dma((GROUP, 4)), dma((GROUP, 4)),
            dma((GROUP, 4)), dma((GROUP, 4)),
            dma((GROUP,)), dma((GROUP,)),
            dma((HEADS,)), dma((HEADS,)),
            dma((4,)),
        ],
        compiler_params=pltpu.CompilerParams(
            collective_id=0, has_side_effects=True, vmem_limit_bytes=60 * 1024 * 1024
        ),
    )(
        hidden_patch_vectors.reshape(cams, patches, local_width),
        entry_rms_multiplier.reshape(HEADS, 1, DEPTH),
        lookup_projection_matrix.transpose(1, 0, 2),
        exit_projection_matrix,
        probe_sharpness,
        adjacent_camera_pairs.T,
        prior_frame_allowed.T,
    )
    return result.reshape(frames, cams, patches, local_width)


def solution(mesh):
    placed = (
        P("camtime", None, None, "heads"),
        P(),
        P(None, None, "heads"),
        P("heads", None),
        P("heads"),
        P(),
        P(),
    )
    return jax.shard_map(
        on_device,
        mesh=mesh,
        in_specs=placed,
        out_specs=P("camtime", None, None, "heads"),
        check_vma=False,
    )
```

```python
import jax
import jax.numpy as jnp
from jax import lax
from jax.experimental import pallas as pl
from jax.experimental.pallas import tpu as pltpu
from jax.sharding import PartitionSpec as P

HEADS = 16
ROW = 4
PLANES = 8
GROUP = 3
DEPTH = 128
PATCH = 128
WIDTH = HEADS * DEPTH
ROWS = 2 * PATCH
MASKED = -3e38
LOWEST = -1e30
LOG2E = 1.4426950408889634
SINGLE_SEMS = 14
PART = 4 * DEPTH
UP = (3, 4, 4)
DOWN = (4, 3, 3)


def unit_rows(raw):
    return raw * lax.rsqrt(jnp.mean(raw * raw, axis=-1, keepdims=True) + 1e-06)


def kernel(
    x_hbm, gain_hbm, w_hbm, e_hbm, sharp_ref, adj_ref, allowed_ref, out_ref,
    xg, mg, mstage, kv, kc, gain_ref, w_both, e_both, scaled, x_part, x_land, m_part, m_land, m_own,
    raw_ref, qt, top_ref, total_ref, acc_ref,
    x_recv, x_part_recv, m_recv, m_part_recv, up_recv, dn_recv, sems,
):
    (x_send, x_part_send, m_send, m_part_send, up_send, dn_send, c_recv, c_send,
     e_recv, e_send, w_load, w_recv, w_send, gain_sem) = [sems.at[n] for n in range(SINGLE_SEMS)]
    t = lax.axis_index("camtime")
    h = lax.axis_index("heads")
    z, j = t // 2, t % 2
    a, y, p = h // 8, (h // 2) % ROW, h % 2

    def head(a_, y_, p_):
        return a_ * 8 + y_ * 2 + p_

    rows = [y, (y + 1) % ROW, (y + 3) % ROW, (y + 2) % ROW]
    h_sib = head(a, y, 1 - p)
    t_x = z * 2 + 1 - j
    t_up = ((z + 1) % PLANES) * 2 + j
    t_dn = ((z + PLANES - 1) % PLANES) * 2 + j
    mine = GROUP * j
    theirs = GROUP * (1 - j)

    def remote(src, dst, send, recv, heads=None, camtime=None):
        return pltpu.make_async_remote_copy(
            src_ref=src, dst_ref=dst, send_sem=send, recv_sem=recv,
            device_id={"camtime": t if camtime is None else camtime, "heads": h if heads is None else heads},
            device_id_type=pl.DeviceIdType.MESH,
        )

    def arrived(ref, sem):
        pltpu.make_async_copy(ref, ref, sem).wait()

    barrier = pltpu.get_barrier_semaphore()

    def greet(camtime, heads):
        pl.semaphore_signal(
            barrier, inc=1, device_id={"camtime": camtime, "heads": heads}, device_id_type=pl.DeviceIdType.MESH
        )

    for other in range(2, HEADS, 2):
        greet(t, (h + other) % HEADS)
    for other in range(0, HEADS, 2):
        greet(t_x, (h + other) % HEADS)
    greet(t, h_sib)
    greet(t_up, h)
    greet(t_dn, h)

    frame_of = (1 - j, j)

    def x_slot(c, pos, a_, y_):
        return ((c * 2 + pos) * 2 + a_) * ROW + y_

    def m_slot(cam, a_, y_):
        return (cam * 2 + a_) * ROW + y_

    for c in range(GROUP):
        pltpu.make_async_copy(x_hbm.at[mine + c], xg.at[x_slot(c, 1, a, y)], x_recv.at[c, 1]).start()
    gain_load = pltpu.make_async_copy(gain_hbm.at[:, p], gain_ref, gain_sem)
    gain_load.start()
    for i in range(3):
        pltpu.make_async_copy(w_hbm.at[i, :, p], w_both.at[:, :, i * DEPTH:(i + 1) * DEPTH], w_load).start()
    for c in range(GROUP):
        top_ref[c] = jnp.full((1, ROWS), LOWEST, jnp.float32)
        total_ref[c] = jnp.zeros((1, ROWS), jnp.float32)
        acc_ref[c] = jnp.zeros((DEPTH, ROWS), jnp.float32)
    pl.semaphore_wait(barrier, HEADS + 2)

    chips = [(a_, y_) for y_ in rows for a_ in (1 - a, a)]

    def x_push(c):
        for a_, y_ in chips:
            remote(x_hbm.at[theirs + c], xg.at[x_slot(c, 0, a, y)], x_send, x_recv.at[c, 0],
                   heads=head(a_, y_, p), camtime=t_x).start()
        for n, (a_, y_) in enumerate(chips):
            if n != 1:
                remote(x_hbm.at[mine + c], xg.at[x_slot(c, 1, a, y)], x_send, x_recv.at[c, 1],
                       heads=head(a_, y_, p)).start()

    def w_copy(i):
        return remote(
            w_hbm.at[i, :, 1 - p], w_both.at[:, :, (3 + i) * DEPTH:(4 + i) * DEPTH], w_send, w_recv, heads=h_sib
        )

    def e_push():
        for n, (a_, y_) in enumerate(chips):
            for side, p_ in enumerate((p, 1 - p)):
                src = e_hbm.at[:, pl.ds(pl.multiple_of(head(a_, y_, p_) * DEPTH, DEPTH), DEPTH)]
                dst = e_both.at[a * ROW + y, :, side * DEPTH:(side + 1) * DEPTH]
                if n == 1:
                    pltpu.make_async_copy(src, dst, e_recv).start()
                else:
                    remote(src, dst, e_send, e_recv, heads=head(a_, y_, p)).start()

    scale = sharp_ref[0] * (LOG2E / DEPTH**0.5)

    def up_copy(c, pos, d):
        src = kc.at[mine + c, frame_of[pos]] if d == 0 else kv.at[z - d, c, pos]
        return remote(src, kv.at[z - d, c, pos], up_send, up_recv.at[c, pos, d], camtime=t_up)

    def dn_copy(c, pos, hop):
        plane = (z + hop) % PLANES
        src = kc.at[mine + c, frame_of[pos]] if hop == 0 else kv.at[plane, c, pos]
        return remote(src, kv.at[plane, c, pos], dn_send, dn_recv.at[c, pos, hop], camtime=t_dn)

    def cross_copy(c):
        return remote(kc.at[mine + c], kc.at[mine + c], c_send, c_recv, camtime=t_x)

    def part_copy(c, places):
        lo, count = places[0], len(places)
        return remote(
            x_part.at[c, pl.ds(lo, count)], x_land.at[c, pl.ds(lo, count)],
            x_part_send, x_part_recv.at[c, lo], heads=h_sib,
        )

    def project_half(c, places):
        count = len(places) * PATCH
        squares = jnp.zeros((count, DEPTH), jnp.float32)
        for pos in places:
            arrived(xg.at[pl.ds(x_slot(c, pos, 0, 0), HEADS // 2)], x_recv.at[c, pos])
        for n in range(HEADS // 2):
            wide = jnp.concatenate([xg[x_slot(c, pos, 0, n)] for pos in places], axis=0).astype(jnp.float32)
            squares = squares + wide * wide
            scaled[:count, n * DEPTH:(n + 1) * DEPTH] = (wide * gain_ref[n]).astype(jnp.bfloat16)
        part = jnp.dot(
            scaled[:count], w_both[...].reshape(WIDTH // 2, 6 * DEPTH), preferred_element_type=jnp.float32
        )
        for n, pos in enumerate(places):
            here = slice(n * PATCH, (n + 1) * PATCH)
            x_part[c, pos, :, :3 * DEPTH] = part[here, 3 * DEPTH:]
            x_part[c, pos, :, 3 * DEPTH:] = squares[here]
            raw_ref[c, pos] = part[here, :3 * DEPTH]
        part_copy(c, places).start()

    def project(c, places):
        lo, count = places[0], len(places)
        arrived(x_land.at[c, pl.ds(lo, count)], x_part_recv.at[c, lo])
        land = x_land[c, lo:lo + count].reshape(count * PATCH, PART)
        squares = x_part[c, lo:lo + count].reshape(count * PATCH, PART)[:, 3 * DEPTH:] + land[:, 3 * DEPTH:]
        inv_rms = lax.rsqrt(jnp.sum(squares, axis=1, keepdims=True) / WIDTH + 1e-06)
        raw = (raw_ref[c, lo:lo + count].reshape(count * PATCH, 3 * DEPTH) + land[:, :3 * DEPTH]) * inv_rms
        key = unit_rows(raw[:, DEPTH:2 * DEPTH]).astype(jnp.bfloat16)
        value = raw[:, 2 * DEPTH:]
        for n, pos in enumerate(places):
            kc[mine + c, frame_of[pos], 0] = key[n * PATCH:(n + 1) * PATCH]
            kc[mine + c, frame_of[pos], 1] = value[n * PATCH:(n + 1) * PATCH].T.astype(jnp.bfloat16)

            @pl.when(z < PLANES - 1)
            def _():
                up_copy(c, pos, 0).start()

            @pl.when(z < DOWN[c])
            def _():
                dn_copy(c, pos, 0).start()

        if 1 in places:
            cross_copy(c).start()
        query = unit_rows(raw[:, :DEPTH])
        for n, pos in enumerate(places):
            qt[c, :, pos * PATCH:(pos + 1) * PATCH] = query[n * PATCH:(n + 1) * PATCH].T.astype(jnp.bfloat16)

    def bias(plane, f, c, later=True):
        return jnp.where((allowed_ref[mine + c, 2 * plane + f] == 1) & later, 0.0, MASKED).astype(jnp.float32)

    def fold(c, score, values, lanes):
        before = top_ref[c, :, lanes]
        top = jnp.maximum(before, jnp.max(score, axis=0, keepdims=True))
        expo = jnp.exp2(score - top)
        rescale = jnp.exp2(before - top)
        top_ref[c, :, lanes] = top
        total_ref[c, :, lanes] = total_ref[c, :, lanes] * rescale + jnp.sum(expo, axis=0, keepdims=True)
        acc_ref[c, :, lanes] = acc_ref[c, :, lanes] * rescale + jnp.dot(
            values, expo.astype(jnp.bfloat16), preferred_element_type=jnp.float32
        )

    def attend(c, plane):
        keys = jnp.concatenate([kv[plane, c, 0, 0], kv[plane, c, 1, 0]], axis=0)
        values = jnp.concatenate([kv[plane, c, 0, 1], kv[plane, c, 1, 1]], axis=1)
        score = jnp.dot(keys, qt[c], preferred_element_type=jnp.float32) * scale
        score = jnp.concatenate(
            [score[:PATCH] + bias(plane, frame_of[0], c), score[PATCH:] + bias(plane, frame_of[1], c)], axis=0
        )
        fold(c, score, values, slice(0, ROWS))

    def attend_cross(c):
        if c == 0:
            arrived(kc.at[pl.ds(theirs, GROUP)], c_recv)
        cam = mine + c
        for pos, f in enumerate(frame_of):
            lanes = slice(pos * PATCH, (pos + 1) * PATCH)
            near = [(cam, f), (adj_ref[0, cam], f), (adj_ref[1, cam], f), (cam, 0)]
            keys = jnp.concatenate([kc[n, f_, 0] for n, f_ in near], axis=0)
            values = jnp.concatenate([kc[n, f_, 1] for n, f_ in near], axis=1)
            score = jnp.dot(keys, qt[c, :, lanes], preferred_element_type=jnp.float32) * scale
            score = jnp.concatenate(
                [score[:3 * PATCH], score[3 * PATCH:] + bias(z, 0, c, f == 1)], axis=0
            )
            fold(c, score, values, lanes)

    def step_up(c, d):
        @pl.when(z >= d)
        def _():
            for pos in range(2):
                arrived(kv.at[z - d, c, pos], up_recv.at[c, pos, d - 1])
                if d < UP[c]:
                    @pl.when(z < PLANES - 1)
                    def _():
                        up_copy(c, pos, d).start()
            attend(c, z - d)

    def step_dn(c, hop):
        plane = (z + hop) % PLANES

        @pl.when(plane < DOWN[c])
        def _():
            for pos in range(2):
                arrived(kv.at[plane, c, pos], dn_recv.at[c, pos, hop - 1])
                if hop < DOWN[c]:
                    dn_copy(c, pos, hop).start()

            @pl.when(plane < z)
            def _():
                attend(c, plane)

    def m_push(c):
        mixed = (acc_ref[c] / total_ref[c]).T.astype(jnp.bfloat16).reshape(2, PATCH, DEPTH)
        mstage[c] = mixed
        cam = mine + c
        slot = m_slot(cam, a, y)
        for a_, y_ in chips:
            remote(mstage.at[c, 0], mg.at[slot], m_send, m_recv.at[c], heads=head(a_, y_, p), camtime=t_x).start()
        for n, (a_, y_) in enumerate(chips):
            if n != 1:
                remote(mstage.at[c, 1], mg.at[slot], m_send, m_recv.at[c], heads=head(a_, y_, p)).start()
        mg[slot] = mstage[c, 1]

    def m_copy(c):
        return remote(m_part.at[c], m_land.at[c], m_part_send, m_part_recv.at[c], heads=h_sib)

    def project_out_half(c):
        arrived(xg.at[pl.ds(0, HEADS - 1)], m_recv.at[c])
        summed = jnp.zeros((ROWS, 2 * DEPTH), jnp.float32)
        for n in range(HEADS // 2):
            mixed = jnp.concatenate([mg[m_slot(cam, 0, n)] for cam in (mine + c, theirs + c)], axis=0)
            part = jnp.dot(mixed, e_both[n], preferred_element_type=jnp.float32)
            summed = summed + part.astype(jnp.bfloat16).astype(jnp.float32)
        m_part[c] = summed[:, DEPTH:]
        m_copy(c).start()
        m_own[c] = summed[:, :DEPTH]

    def project_out(c):
        arrived(m_land.at[c], m_part_recv.at[c])
        summed = (m_own[c] + m_land[c]).astype(jnp.bfloat16)
        out_ref[mine + c] = summed[:PATCH]
        out_ref[theirs + c] = summed[PATCH:]

    x_push(0)
    for i in range(3):
        w_copy(i).start()
    x_push(1)
    x_push(2)
    gain_load.wait()
    arrived(w_both.at[:, :, :3 * DEPTH], w_load)
    arrived(w_both.at[:, :, 3 * DEPTH:], w_recv)
    project_half(0, (0,))
    project(0, (0,))
    project_half(0, (1,))
    project(0, (1,))
    project_half(1, (0,))
    step_up(0, 1)
    step_dn(0, 1)
    project_half(1, (1,))
    project(1, (0,))
    project(1, (1,))
    project_half(2, (0,))
    step_up(0, 2)
    project(2, (0,))
    project_half(2, (1,))
    step_dn(0, 2)
    step_up(1, 1)
    project(2, (1,))
    e_push()
    step_dn(1, 1)
    step_dn(0, 3)
    step_up(1, 2)
    step_dn(1, 2)
    step_up(2, 1)
    step_dn(2, 1)
    attend_cross(0)
    step_up(0, 3)
    step_dn(0, 4)
    m_push(0)
    attend_cross(1)
    step_up(1, 3)
    step_up(2, 2)
    step_dn(1, 3)
    attend_cross(2)
    step_up(1, 4)
    step_dn(2, 2)
    m_push(1)
    step_up(2, 3)
    step_dn(2, 3)
    step_up(2, 4)
    m_push(2)
    arrived(e_both, e_recv)
    project_out_half(0)
    project_out_half(1)
    project_out(0)
    project_out(1)
    project_out_half(2)
    project_out(2)

    pieces = HEADS - 1
    arrived(xg.at[pl.ds(0, GROUP * pieces)], x_send)
    arrived(xg.at[pl.ds(0, GROUP * pieces)], m_send)
    arrived(xg.at[pl.ds(0, HEADS - 2)], e_send)
    arrived(xg.at[pl.ds(0, 3 * HEADS // 2)], w_send)
    arrived(x_part, x_part_send)
    arrived(m_part, m_part_send)
    arrived(kc.at[pl.ds(mine, GROUP)], c_send)
    for plane in range(PLANES):
        ups = sum(min(UP[c], plane + 1) for c in range(GROUP)) if plane < PLANES - 1 else 0
        downs = sum((plane + hop) % PLANES < DOWN[c] for c in range(GROUP) for hop in range(DOWN[c]))

        @pl.when(z == plane)
        def _():
            if ups:
                arrived(xg.at[pl.ds(0, 4 * ups)], up_send)
            if downs:
                arrived(xg.at[pl.ds(0, 4 * downs)], dn_send)


def on_device(
    hidden_patch_vectors,
    entry_rms_multiplier,
    lookup_projection_matrix,
    exit_projection_matrix,
    probe_sharpness,
    adjacent_camera_pairs,
    prior_frame_allowed,
):
    frames, cams, patches, local_width = hidden_patch_vectors.shape
    vmem = pl.BlockSpec(memory_space=pltpu.VMEM)
    smem = pl.BlockSpec(memory_space=pltpu.SMEM)
    hbm = pl.BlockSpec(memory_space=pltpu.HBM)
    dma = pltpu.SemaphoreType.DMA
    bf16, f32 = jnp.bfloat16, jnp.float32
    result = pl.pallas_call(
        kernel,
        out_shape=jax.ShapeDtypeStruct((cams, patches, local_width), bf16),
        in_specs=[hbm, hbm, hbm, hbm, smem, smem, smem],
        out_specs=vmem,
        scratch_shapes=[
            pltpu.VMEM((GROUP * HEADS, PATCH, DEPTH), bf16),
            pltpu.VMEM((GROUP * HEADS, PATCH, DEPTH), bf16),
            pltpu.VMEM((GROUP, 2, PATCH, DEPTH), bf16),
            pltpu.VMEM((PLANES, GROUP, 2, 2, PATCH, DEPTH), bf16),
            pltpu.VMEM((2 * GROUP, 2, 2, PATCH, DEPTH), bf16),
            pltpu.VMEM((HEADS // 2, 1, DEPTH), f32),
            pltpu.VMEM((HEADS // 2, DEPTH, 6 * DEPTH), bf16),
            pltpu.VMEM((HEADS // 2, DEPTH, 2 * DEPTH), bf16),
            pltpu.VMEM((ROWS, WIDTH // 2), bf16),
            pltpu.VMEM((GROUP, 2, PATCH, PART), f32),
            pltpu.VMEM((GROUP, 2, PATCH, PART), f32),
            pltpu.VMEM((GROUP, ROWS, DEPTH), f32),
            pltpu.VMEM((GROUP, ROWS, DEPTH), f32),
            pltpu.VMEM((GROUP, ROWS, DEPTH), f32),
            pltpu.VMEM((GROUP, 2, PATCH, 3 * DEPTH), f32),
            pltpu.VMEM((GROUP, DEPTH, ROWS), bf16),
            pltpu.VMEM((GROUP, 1, ROWS), f32),
            pltpu.VMEM((GROUP, 1, ROWS), f32),
            pltpu.VMEM((GROUP, DEPTH, ROWS), f32),
            dma((GROUP, 2)),
            dma((GROUP, 2)),
            dma((GROUP,)),
            dma((GROUP,)),
            dma((GROUP, 2, 4)),
            dma((GROUP, 2, 4)),
            dma((SINGLE_SEMS,)),
        ],
        compiler_params=pltpu.CompilerParams(
            collective_id=0, has_side_effects=True, vmem_limit_bytes=60 * 1024 * 1024
        ),
    )(
        hidden_patch_vectors.reshape(cams, patches, local_width),
        entry_rms_multiplier.reshape(HEADS // 2, 2, 1, DEPTH),
        lookup_projection_matrix.transpose(1, 0, 2).reshape(3, HEADS // 2, 2, DEPTH, DEPTH),
        exit_projection_matrix,
        probe_sharpness,
        adjacent_camera_pairs.T,
        prior_frame_allowed.T,
    )
    return result.reshape(frames, cams, patches, local_width)


def solution(mesh):
    placed = (
        P("camtime", None, None, "heads"),
        P(),
        P(None, None, "heads"),
        P("heads", None),
        P("heads"),
        P(),
        P(),
    )
    return jax.shard_map(
        on_device,
        mesh=mesh,
        in_specs=placed,
        out_specs=P("camtime", None, None, "heads"),
        check_vma=False,
    )
```

```python
import jax
import jax.numpy as jnp
from jax import lax
from jax.experimental import pallas as pl
from jax.experimental.pallas import tpu as pltpu
from jax.sharding import PartitionSpec as P

HEADS = 16
ROW = 4
PLANES = 8
GROUP = 3
DEPTH = 128
PATCH = 128
WIDTH = HEADS * DEPTH
ROWS = 2 * PATCH
MASKED = -3e38
LOWEST = -1e30
LOG2E = 1.4426950408889634
SINGLE_SEMS = 18
PART = 4 * DEPTH
UP = ((3, 4), (3, 3), (4, 4))
DOWN = ((4, 3), (4, 4), (3, 3))
TREE_X = (2,)
ORDER = (
    "H00", "P00", "X20", "H01", "P01", "X21", "H10", "U001", "D001", "P10", "H11", "U011",
    "D011", "P11", "H20", "U101", "U002", "D002", "D101", "U012", "P20", "H21",
    "D012", "U003", "D111", "D003", "P21", "E", "D102", "U013", "D013", "C0",
    "U111", "C2", "U201", "C1", "D112", "D201", "D004", "U102", "U014", "F0",
    "U211", "U112", "D103", "D113", "D211", "U202", "U103", "D104", "U212", "D202",
    "U113", "D114", "F1", "U203", "D212", "U213", "D203", "U204", "D213", "U214",
    "F2",
)


def unit_rows(raw):
    return raw * lax.rsqrt(jnp.mean(raw * raw, axis=-1, keepdims=True) + 1e-06)


def kernel(
    x_hbm, gain_hbm, w_hbm, e_hbm, sharp_hbm, adj_hbm, allowed_hbm, out_hbm,
    xg, mg, mstage, kv, kc, gain_ref, w_both, e_both, scaled, x_part, x_land, m_part, m_land, m_own,
    raw_ref, qt, top_ref, total_ref, acc_ref, out_ref, sharp_ref, adj_ref, allowed_ref,
    x_recv, x_row, x_part_recv, m_recv, m_part_recv, up_recv, dn_recv, sems,
):
    (x_send, x_part_send, m_send, m_part_send, up_send, dn_send, c_recv, c_send,
     e_recv, e_send, w_load, w_recv, w_send, gain_sem, sharp_sem, adj_sem, allowed_sem, out_sem) = [sems.at[n] for n in range(SINGLE_SEMS)]
    t = lax.axis_index("camtime")
    h = lax.axis_index("heads")
    z, j = t // 2, t % 2
    a, y, p = h // 8, (h // 2) % ROW, h % 2

    def head(a_, y_, p_):
        return a_ * 8 + y_ * 2 + p_

    rows = [y, (y + 1) % ROW, (y + 3) % ROW, (y + 2) % ROW]
    h_sib = head(a, y, 1 - p)
    t_x = z * 2 + 1 - j
    t_up = ((z + 1) % PLANES) * 2 + j
    t_dn = ((z + PLANES - 1) % PLANES) * 2 + j
    mine = GROUP * j
    theirs = GROUP * (1 - j)

    def remote(src, dst, send, recv, heads=None, camtime=None):
        return pltpu.make_async_remote_copy(
            src_ref=src, dst_ref=dst, send_sem=send, recv_sem=recv,
            device_id={"camtime": t if camtime is None else camtime, "heads": h if heads is None else heads},
            device_id_type=pl.DeviceIdType.MESH,
        )

    def arrived(ref, sem):
        pltpu.make_async_copy(ref, ref, sem).wait()

    barrier = pltpu.get_barrier_semaphore()

    def greet(camtime, heads):
        pl.semaphore_signal(
            barrier, inc=1, device_id={"camtime": camtime, "heads": heads}, device_id_type=pl.DeviceIdType.MESH
        )

    for other in range(2, HEADS, 2):
        greet(t, (h + other) % HEADS)
    for other in range(0, HEADS, 2):
        greet(t_x, (h + other) % HEADS)
    greet(t, h_sib)
    greet(t_up, h)
    greet(t_dn, h)

    frame_of = (1 - j, j)

    def x_slot(c, pos, a_, y_):
        return ((c * 2 + pos) * ROW + y_) * 2 + a_

    def m_slot(cam, a_, y_):
        return (cam * ROW + y_) * 2 + a_

    for c in range(GROUP):
        pltpu.make_async_copy(x_hbm.at[mine + c], xg.at[x_slot(c, 1, a, y)], (x_row if c in TREE_X else x_recv).at[c, 1]).start()
    gain_load = pltpu.make_async_copy(gain_hbm.at[:, p], gain_ref, gain_sem)
    gain_load.start()
    small_loads = [
        pltpu.make_async_copy(sharp_hbm, sharp_ref, sharp_sem),
        pltpu.make_async_copy(adj_hbm, adj_ref, adj_sem),
        pltpu.make_async_copy(allowed_hbm, allowed_ref, allowed_sem),
    ]
    for load in small_loads:
        load.start()
    for i in range(3):
        pltpu.make_async_copy(w_hbm.at[i, :, p], w_both.at[:, :, i * DEPTH:(i + 1) * DEPTH], w_load).start()
    for c in range(GROUP):
        top_ref[c] = jnp.full((1, ROWS), LOWEST, jnp.float32)
        total_ref[c] = jnp.zeros((1, ROWS), jnp.float32)
        acc_ref[c] = jnp.zeros((DEPTH, ROWS), jnp.float32)
    pl.semaphore_wait(barrier, HEADS + 2)

    chips = [(a_, y_) for y_ in rows for a_ in (1 - a, a)]

    def row_push(buf, slot, send, recv):
        for y_ in rows[1:]:
            remote(buf.at[pl.ds(slot, 2)], buf.at[pl.ds(slot, 2)], send, recv, heads=head(a, y_, p)).start()

    def x_push(c):
        if c in TREE_X:
            for a_ in (1 - a, a):
                remote(x_hbm.at[theirs + c], xg.at[x_slot(c, 0, a, y)], x_send, x_row.at[c, 0],
                       heads=head(a_, y, p), camtime=t_x).start()
            remote(x_hbm.at[mine + c], xg.at[x_slot(c, 1, a, y)], x_send, x_row.at[c, 1],
                   heads=head(1 - a, y, p)).start()
            return
        for a_, y_ in chips:
            remote(x_hbm.at[theirs + c], xg.at[x_slot(c, 0, a, y)], x_send, x_recv.at[c, 0],
                   heads=head(a_, y_, p), camtime=t_x).start()
        for n, (a_, y_) in enumerate(chips):
            if n != 1:
                remote(x_hbm.at[mine + c], xg.at[x_slot(c, 1, a, y)], x_send, x_recv.at[c, 1],
                       heads=head(a_, y_, p)).start()

    def x_relay(c, pos):
        slot = x_slot(c, pos, 0, y)
        arrived(xg.at[pl.ds(slot, 2)], x_row.at[c, pos])
        row_push(xg, slot, x_send, x_recv.at[c, pos])

    def w_copy(i):
        return remote(
            w_hbm.at[i, :, 1 - p], w_both.at[:, :, (3 + i) * DEPTH:(4 + i) * DEPTH], w_send, w_recv, heads=h_sib
        )

    def e_push():
        for n, (a_, y_) in enumerate(chips):
            for side, p_ in enumerate((p, 1 - p)):
                src = e_hbm.at[:, pl.ds(pl.multiple_of(head(a_, y_, p_) * DEPTH, DEPTH), DEPTH)]
                dst = e_both.at[a * ROW + y, :, side * DEPTH:(side + 1) * DEPTH]
                if n == 1:
                    pltpu.make_async_copy(src, dst, e_recv).start()
                else:
                    remote(src, dst, e_send, e_recv, heads=head(a_, y_, p)).start()


    def up_copy(c, pos, d):
        src = kc.at[mine + c, frame_of[pos]] if d == 0 else kv.at[z - d, c, pos]
        return remote(src, kv.at[z - d, c, pos], up_send, up_recv.at[c, pos, d], camtime=t_up)

    def dn_copy(c, pos, hop):
        plane = (z + hop) % PLANES
        src = kc.at[mine + c, frame_of[pos]] if hop == 0 else kv.at[plane, c, pos]
        return remote(src, kv.at[plane, c, pos], dn_send, dn_recv.at[c, pos, hop], camtime=t_dn)

    def cross_copy(c):
        return remote(kc.at[mine + c], kc.at[mine + c], c_send, c_recv, camtime=t_x)

    def part_copy(c, places):
        lo, count = places[0], len(places)
        return remote(
            x_part.at[c, pl.ds(lo, count)], x_land.at[c, pl.ds(lo, count)],
            x_part_send, x_part_recv.at[c, lo], heads=h_sib,
        )

    def project_half(c, places):
        count = len(places) * PATCH
        squares = jnp.zeros((count, DEPTH), jnp.float32)
        for pos in places:
            arrived(xg.at[pl.ds(x_slot(c, pos, 0, 0), 6 if c in TREE_X else 8)], x_recv.at[c, pos])
        for n in range(HEADS // 2):
            wide = jnp.concatenate([xg[x_slot(c, pos, n // ROW, n % ROW)] for pos in places], axis=0).astype(jnp.float32)
            squares = squares + wide * wide
            scaled[:count, n * DEPTH:(n + 1) * DEPTH] = (wide * gain_ref[n]).astype(jnp.bfloat16)
        part = jnp.dot(
            scaled[:count], w_both[...].reshape(WIDTH // 2, 6 * DEPTH), preferred_element_type=jnp.float32
        )
        for n, pos in enumerate(places):
            here = slice(n * PATCH, (n + 1) * PATCH)
            x_part[c, pos, :, :3 * DEPTH] = part[here, 3 * DEPTH:]
            x_part[c, pos, :, 3 * DEPTH:] = squares[here]
            raw_ref[c, pos] = part[here, :3 * DEPTH]
        part_copy(c, places).start()

    def project(c, places):
        lo, count = places[0], len(places)
        arrived(x_land.at[c, pl.ds(lo, count)], x_part_recv.at[c, lo])
        land = x_land[c, lo:lo + count].reshape(count * PATCH, PART)
        squares = x_part[c, lo:lo + count].reshape(count * PATCH, PART)[:, 3 * DEPTH:] + land[:, 3 * DEPTH:]
        inv_rms = lax.rsqrt(jnp.sum(squares, axis=1, keepdims=True) / WIDTH + 1e-06)
        raw = (raw_ref[c, lo:lo + count].reshape(count * PATCH, 3 * DEPTH) + land[:, :3 * DEPTH]) * inv_rms
        key = unit_rows(raw[:, DEPTH:2 * DEPTH]).astype(jnp.bfloat16)
        value = raw[:, 2 * DEPTH:]
        for n, pos in enumerate(places):
            kc[mine + c, frame_of[pos], 0] = key[n * PATCH:(n + 1) * PATCH]
            kc[mine + c, frame_of[pos], 1] = value[n * PATCH:(n + 1) * PATCH].T.astype(jnp.bfloat16)

            @pl.when(z < PLANES - 1)
            def _():
                up_copy(c, pos, 0).start()

            @pl.when(z < DOWN[c][pos])
            def _():
                dn_copy(c, pos, 0).start()

        if 1 in places:
            cross_copy(c).start()
        query = unit_rows(raw[:, :DEPTH])
        for n, pos in enumerate(places):
            qt[c, :, pos * PATCH:(pos + 1) * PATCH] = query[n * PATCH:(n + 1) * PATCH].T.astype(jnp.bfloat16)

    def bias(plane, f, c, later=True):
        return jnp.where((allowed_ref[mine + c, 2 * plane + f] == 1) & later, 0.0, MASKED).astype(jnp.float32)

    def fold(c, score, values, lanes):
        before = top_ref[c, :, lanes]
        top = jnp.maximum(before, jnp.max(score, axis=0, keepdims=True))
        expo = jnp.exp2(score - top)
        rescale = jnp.exp2(before - top)
        top_ref[c, :, lanes] = top
        total_ref[c, :, lanes] = total_ref[c, :, lanes] * rescale + jnp.sum(expo, axis=0, keepdims=True)
        acc_ref[c, :, lanes] = acc_ref[c, :, lanes] * rescale + jnp.dot(
            values, expo.astype(jnp.bfloat16), preferred_element_type=jnp.float32
        )

    def attend(c, plane):
        keys = jnp.concatenate([kv[plane, c, 0, 0], kv[plane, c, 1, 0]], axis=0)
        values = jnp.concatenate([kv[plane, c, 0, 1], kv[plane, c, 1, 1]], axis=1)
        score = jnp.dot(keys, qt[c], preferred_element_type=jnp.float32) * (sharp_ref[0, 0] * (LOG2E / DEPTH**0.5))
        score = jnp.concatenate(
            [score[:PATCH] + bias(plane, frame_of[0], c), score[PATCH:] + bias(plane, frame_of[1], c)], axis=0
        )
        fold(c, score, values, slice(0, ROWS))

    crossed = []

    def attend_cross(c):
        if not crossed:
            crossed.append(c)
            arrived(kc.at[pl.ds(theirs, GROUP)], c_recv)
        cam = mine + c
        for pos, f in enumerate(frame_of):
            lanes = slice(pos * PATCH, (pos + 1) * PATCH)
            near = [(cam, f), (adj_ref[0, cam], f), (adj_ref[1, cam], f), (cam, 0)]
            keys = jnp.concatenate([kc[n, f_, 0] for n, f_ in near], axis=0)
            values = jnp.concatenate([kc[n, f_, 1] for n, f_ in near], axis=1)
            score = jnp.dot(keys, qt[c, :, lanes], preferred_element_type=jnp.float32) * (sharp_ref[0, 0] * (LOG2E / DEPTH**0.5))
            score = jnp.concatenate(
                [score[:3 * PATCH], score[3 * PATCH:] + bias(z, 0, c, f == 1)], axis=0
            )
            fold(c, score, values, lanes)

    deliveries = {}
    for n, step in enumerate(ORDER):
        if step[0] in "UD":
            below = int(step[3]) if step[0] == "U" else PLANES - int(step[3])
            deliveries[step[1], below] = n

    def step_up(n, c, pos, d):
        @pl.when(z >= d)
        def _():
            arrived(kv.at[z - d, c, pos], up_recv.at[c, pos, d - 1])
            if d < UP[c][pos]:
                @pl.when(z < PLANES - 1)
                def _():
                    up_copy(c, pos, d).start()
            if deliveries[str(c), d] == n:
                attend(c, z - d)

    def step_dn(n, c, pos, hop):
        plane = (z + hop) % PLANES

        @pl.when(plane < DOWN[c][pos])
        def _():
            arrived(kv.at[plane, c, pos], dn_recv.at[c, pos, hop - 1])
            if hop < DOWN[c][pos]:
                dn_copy(c, pos, hop).start()
            if deliveries[str(c), PLANES - hop] == n:
                @pl.when(plane < z)
                def _():
                    attend(c, plane)

    def m_push(c):
        mixed = (acc_ref[c] / total_ref[c]).T.astype(jnp.bfloat16).reshape(2, PATCH, DEPTH)
        mstage[c] = mixed
        cam = mine + c
        slot = m_slot(cam, a, y)
        mg[slot] = mstage[c, 1]
        for a_, y_ in chips:
            remote(mstage.at[c, 0], mg.at[slot], m_send, m_recv.at[c], heads=head(a_, y_, p), camtime=t_x).start()
        for n, (a_, y_) in enumerate(chips):
            if n != 1:
                remote(mstage.at[c, 1], mg.at[slot], m_send, m_recv.at[c], heads=head(a_, y_, p)).start()

    def m_copy(c):
        return remote(m_part.at[c], m_land.at[c], m_part_send, m_part_recv.at[c], heads=h_sib)

    def project_out_half(c):
        arrived(xg.at[pl.ds(0, HEADS - 1)], m_recv.at[c])
        summed = jnp.zeros((ROWS, 2 * DEPTH), jnp.float32)
        for n in range(HEADS // 2):
            mixed = jnp.concatenate([mg[m_slot(cam, n // ROW, n % ROW)] for cam in (mine + c, theirs + c)], axis=0)
            part = jnp.dot(mixed, e_both[n], preferred_element_type=jnp.float32)
            summed = summed + part.astype(jnp.bfloat16).astype(jnp.float32)
        m_part[c] = summed[:, DEPTH:]
        m_copy(c).start()
        m_own[c] = summed[:, :DEPTH]

    def project_out(c):
        arrived(m_land.at[c], m_part_recv.at[c])
        summed = (m_own[c] + m_land[c]).astype(jnp.bfloat16)
        out_ref[mine + c] = summed[:PATCH]
        out_ref[theirs + c] = summed[PATCH:]
        for cam in (mine + c, theirs + c):
            pltpu.make_async_copy(out_ref.at[cam], out_hbm.at[cam], out_sem).start()

    x_push(0)
    for i in range(3):
        w_copy(i).start()
    for c in TREE_X:
        x_push(c)
    for c in range(1, GROUP):
        if c not in TREE_X:
            x_push(c)
    for load in [gain_load] + small_loads:
        load.wait()
    arrived(w_both.at[:, :, :3 * DEPTH], w_load)
    arrived(w_both.at[:, :, 3 * DEPTH:], w_recv)
    for n, step in enumerate(ORDER):
        kind, c = step[0], int(step[1:2] or 0)
        pos, hop = int(step[2:3] or 0), int(step[3:] or 0)
        if kind == "H":
            project_half(c, (pos,))
        elif kind == "P":
            project(c, (pos,))
        elif kind == "U":
            step_up(n, c, pos, hop)
        elif kind == "D":
            step_dn(n, c, pos, hop)
        elif kind == "C":
            attend_cross(c)
        elif kind == "F":
            m_push(c)
        elif kind == "X":
            if c in TREE_X:
                x_relay(c, pos)
        else:
            e_push()
    arrived(e_both, e_recv)
    project_out_half(0)
    project_out_half(1)
    project_out(0)
    project_out(1)
    project_out_half(2)
    project_out(2)

    arrived(out_ref, out_sem)
    pieces = HEADS - 1
    arrived(xg.at[pl.ds(0, GROUP * pieces)], x_send)
    arrived(xg.at[pl.ds(0, GROUP * pieces)], m_send)
    arrived(xg.at[pl.ds(0, HEADS - 2)], e_send)
    arrived(xg.at[pl.ds(0, 3 * HEADS // 2)], w_send)
    arrived(x_part, x_part_send)
    arrived(m_part, m_part_send)
    arrived(kc.at[pl.ds(mine, GROUP)], c_send)
    for plane in range(PLANES):
        frames = [(c, pos) for c in range(GROUP) for pos in range(2)]
        ups = sum(min(UP[c][pos], plane + 1) for c, pos in frames) if plane < PLANES - 1 else 0
        downs = sum((plane + hop) % PLANES < DOWN[c][pos] for c, pos in frames for hop in range(DOWN[c][pos]))

        @pl.when(z == plane)
        def _():
            if ups:
                arrived(xg.at[pl.ds(0, 2 * ups)], up_send)
            if downs:
                arrived(xg.at[pl.ds(0, 2 * downs)], dn_send)


def on_device(
    hidden_patch_vectors,
    entry_rms_multiplier,
    lookup_projection_matrix,
    exit_projection_matrix,
    probe_sharpness,
    adjacent_camera_pairs,
    prior_frame_allowed,
):
    frames, cams, patches, local_width = hidden_patch_vectors.shape
    hbm = pl.BlockSpec(memory_space=pltpu.HBM)
    dma = pltpu.SemaphoreType.DMA
    bf16, f32 = jnp.bfloat16, jnp.float32
    result = pl.pallas_call(
        kernel,
        out_shape=jax.ShapeDtypeStruct((cams, patches, local_width), bf16),
        in_specs=[hbm] * 7,
        out_specs=pl.BlockSpec(memory_space=pltpu.VMEM),
        scratch_shapes=[
            pltpu.VMEM((GROUP * HEADS, PATCH, DEPTH), bf16),
            pltpu.VMEM((GROUP * HEADS, PATCH, DEPTH), bf16),
            pltpu.VMEM((GROUP, 2, PATCH, DEPTH), bf16),
            pltpu.VMEM((PLANES, GROUP, 2, 2, PATCH, DEPTH), bf16),
            pltpu.VMEM((2 * GROUP, 2, 2, PATCH, DEPTH), bf16),
            pltpu.VMEM((HEADS // 2, 1, DEPTH), f32),
            pltpu.VMEM((HEADS // 2, DEPTH, 6 * DEPTH), bf16),
            pltpu.VMEM((HEADS // 2, DEPTH, 2 * DEPTH), bf16),
            pltpu.VMEM((ROWS, WIDTH // 2), bf16),
            pltpu.VMEM((GROUP, 2, PATCH, PART), f32),
            pltpu.VMEM((GROUP, 2, PATCH, PART), f32),
            pltpu.VMEM((GROUP, ROWS, DEPTH), f32),
            pltpu.VMEM((GROUP, ROWS, DEPTH), f32),
            pltpu.VMEM((GROUP, ROWS, DEPTH), f32),
            pltpu.VMEM((GROUP, 2, PATCH, 3 * DEPTH), f32),
            pltpu.VMEM((GROUP, DEPTH, ROWS), bf16),
            pltpu.VMEM((GROUP, 1, ROWS), f32),
            pltpu.VMEM((GROUP, 1, ROWS), f32),
            pltpu.VMEM((GROUP, DEPTH, ROWS), f32),
            pltpu.VMEM((cams, patches, local_width), bf16),
            pltpu.SMEM((1, 1), f32),
            pltpu.SMEM((2, cams), jnp.int32),
            pltpu.SMEM((cams, PLANES * 2), jnp.int32),
            dma((GROUP, 2)),
            dma((GROUP, 2)),
            dma((GROUP, 2)),
            dma((GROUP,)),
            dma((GROUP,)),
            dma((GROUP, 2, 4)),
            dma((GROUP, 2, 4)),
            dma((SINGLE_SEMS,)),
        ],
        compiler_params=pltpu.CompilerParams(
            collective_id=0, has_side_effects=True, vmem_limit_bytes=48 * 1024 * 1024
        ),
    )(*[operand if operand.size == 1 else pltpu.with_memory_space_constraint(operand, pltpu.HBM) for operand in (
        hidden_patch_vectors.reshape(cams, patches, local_width),
        entry_rms_multiplier.reshape(HEADS // 2, 2, 1, DEPTH),
        lookup_projection_matrix.transpose(1, 0, 2).reshape(3, HEADS // 2, 2, DEPTH, DEPTH),
        exit_projection_matrix,
        probe_sharpness.reshape(1, 1),
        adjacent_camera_pairs.T,
        prior_frame_allowed.T,
    )])
    return result.reshape(frames, cams, patches, local_width)


def solution(mesh):
    placed = (
        P("camtime", None, None, "heads"),
        P(),
        P(None, None, "heads"),
        P("heads", None),
        P("heads"),
        P(),
        P(),
    )
    return jax.shard_map(
        on_device,
        mesh=mesh,
        in_specs=placed,
        out_specs=P("camtime", None, None, "heads"),
        check_vma=False,
    )
```

```python
import jax
import jax.numpy as jnp
from jax import lax
from jax.experimental import pallas as pl
from jax.experimental.pallas import tpu as pltpu
from jax.sharding import PartitionSpec as P

HEADS = 16
ROW = 4
PLANES = 8
GROUP = 3
DEPTH = 128
PATCH = 128
WIDTH = HEADS * DEPTH
ROWS = 2 * PATCH
MASKED = -3e38
LOWEST = -1e30
LOG2E = 1.4426950408889634
SINGLE_SEMS = 18
PART = 4 * DEPTH
UP = ((3, 4), (3, 3), (4, 4))
DOWN = ((4, 3), (4, 4), (3, 3))
TREE_X = (2,)
ORDER = (
    "H00", "P00", "H01", "P01", "X20", "H10", "X21", "U001", "D001", "P10", "H11", "U011",
    "D011", "P11", "H20", "U101", "U002", "D002", "D101", "U012", "P20", "H21",
    "D012", "U003", "D111", "D003", "P21", "E", "D102", "U013", "D013",
    "U111", "U201", "D112", "D201", "D004", "C0", "U102", "U014", "F0",
    "C1", "U211", "C2", "U112", "D103", "D113", "D211", "U202", "U103", "D104", "U212", "D202",
    "U113", "D114", "F1", "U203", "D212", "U213", "D203", "U204", "D213", "U214",
    "F2",
)


def unit_rows(raw):
    return raw * lax.rsqrt(jnp.mean(raw * raw, axis=-1, keepdims=True) + 1e-06)


def kernel(
    x_hbm, gain_hbm, w_hbm, e_hbm, sharp_hbm, adj_hbm, allowed_hbm, out_ref,
    xg, mg, mstage, kv, kc, gain_ref, w_both, e_both, scaled, x_part, x_land, m_part, m_land, m_own,
    raw_ref, qt, top_ref, total_ref, acc_ref, sharp_ref, adj_ref, allowed_ref,
    x_recv, x_row, x_part_recv, m_recv, m_part_recv, up_recv, dn_recv, sems,
):
    (x_send, x_part_send, m_send, m_part_send, up_send, dn_send, c_recv, c_send,
     e_recv, e_send, w_load, w_recv, w_send, gain_sem, sharp_sem, adj_sem, allowed_sem, out_sem) = [sems.at[n] for n in range(SINGLE_SEMS)]
    t = lax.axis_index("camtime")
    h = lax.axis_index("heads")
    z, j = t // 2, t % 2
    a, y, p = h // 8, (h // 2) % ROW, h % 2

    def head(a_, y_, p_):
        return a_ * 8 + y_ * 2 + p_

    rows = [y, (y + 1) % ROW, (y + 3) % ROW, (y + 2) % ROW]
    h_sib = head(a, y, 1 - p)
    t_x = z * 2 + 1 - j
    t_up = ((z + 1) % PLANES) * 2 + j
    t_dn = ((z + PLANES - 1) % PLANES) * 2 + j
    mine = GROUP * j
    theirs = GROUP * (1 - j)

    def remote(src, dst, send, recv, heads=None, camtime=None):
        return pltpu.make_async_remote_copy(
            src_ref=src, dst_ref=dst, send_sem=send, recv_sem=recv,
            device_id={"camtime": t if camtime is None else camtime, "heads": h if heads is None else heads},
            device_id_type=pl.DeviceIdType.MESH,
        )

    def arrived(ref, sem):
        pltpu.make_async_copy(ref, ref, sem).wait()

    barrier = pltpu.get_barrier_semaphore()

    def greet(camtime, heads):
        pl.semaphore_signal(
            barrier, inc=1, device_id={"camtime": camtime, "heads": heads}, device_id_type=pl.DeviceIdType.MESH
        )

    for other in range(2, HEADS, 2):
        greet(t, (h + other) % HEADS)
    for other in range(0, HEADS, 2):
        greet(t_x, (h + other) % HEADS)
    greet(t, h_sib)
    greet(t_up, h)
    greet(t_dn, h)

    frame_of = (1 - j, j)

    def x_slot(c, pos, a_, y_):
        return ((c * 2 + pos) * ROW + y_) * 2 + a_

    def m_slot(cam, a_, y_):
        return (cam * ROW + y_) * 2 + a_

    for c in range(GROUP):
        pltpu.make_async_copy(x_hbm.at[mine + c], xg.at[x_slot(c, 1, a, y)], (x_row if c in TREE_X else x_recv).at[c, 1]).start()
    gain_load = pltpu.make_async_copy(gain_hbm.at[:, p], gain_ref, gain_sem)
    gain_load.start()
    small_loads = [
        pltpu.make_async_copy(sharp_hbm, sharp_ref, sharp_sem),
        pltpu.make_async_copy(adj_hbm, adj_ref, adj_sem),
        pltpu.make_async_copy(allowed_hbm, allowed_ref, allowed_sem),
    ]
    for load in small_loads:
        load.start()
    for i in range(3):
        pltpu.make_async_copy(w_hbm.at[i, :, p], w_both.at[:, :, i * DEPTH:(i + 1) * DEPTH], w_load).start()
    for c in range(GROUP):
        top_ref[c] = jnp.full((1, ROWS), LOWEST, jnp.float32)
        total_ref[c] = jnp.zeros((1, ROWS), jnp.float32)
        acc_ref[c] = jnp.zeros((DEPTH, ROWS), jnp.float32)
    pl.semaphore_wait(barrier, HEADS + 2)

    near = [(a_, y_) for y_ in rows for a_ in (1 - a, a)]
    self_chip = near[1]
    chips = near[6:8] + near[2:6] + near[0:2]

    def row_push(buf, slot, send, recv):
        for y_ in rows[1:]:
            remote(buf.at[pl.ds(slot, 2)], buf.at[pl.ds(slot, 2)], send, recv, heads=head(a, y_, p)).start()

    def x_push(c):
        if c in TREE_X:
            for a_ in (1 - a, a):
                remote(x_hbm.at[theirs + c], xg.at[x_slot(c, 0, a, y)], x_send, x_row.at[c, 0],
                       heads=head(a_, y, p), camtime=t_x).start()
            remote(x_hbm.at[mine + c], xg.at[x_slot(c, 1, a, y)], x_send, x_row.at[c, 1],
                   heads=head(1 - a, y, p)).start()
            return
        for chip in chips:
            a_, y_ = chip
            remote(x_hbm.at[theirs + c], xg.at[x_slot(c, 0, a, y)], x_send, x_recv.at[c, 0],
                   heads=head(a_, y_, p), camtime=t_x).start()
        for chip in chips:
            a_, y_ = chip
            if chip is not self_chip:
                remote(x_hbm.at[mine + c], xg.at[x_slot(c, 1, a, y)], x_send, x_recv.at[c, 1],
                       heads=head(a_, y_, p)).start()

    def x_relay(c, pos):
        slot = x_slot(c, pos, 0, y)
        arrived(xg.at[pl.ds(slot, 2)], x_row.at[c, pos])
        row_push(xg, slot, x_send, x_recv.at[c, pos])

    def w_copy(i):
        return remote(
            w_hbm.at[i, :, 1 - p], w_both.at[:, :, (3 + i) * DEPTH:(4 + i) * DEPTH], w_send, w_recv, heads=h_sib
        )

    def e_push():
        for chip in chips:
            a_, y_ = chip
            for side, p_ in enumerate((p, 1 - p)):
                src = e_hbm.at[:, pl.ds(pl.multiple_of(head(a_, y_, p_) * DEPTH, DEPTH), DEPTH)]
                dst = e_both.at[a * ROW + y, :, side * DEPTH:(side + 1) * DEPTH]
                if chip is self_chip:
                    pltpu.make_async_copy(src, dst, e_recv).start()
                else:
                    remote(src, dst, e_send, e_recv, heads=head(a_, y_, p)).start()


    def up_copy(c, pos, d):
        src = kc.at[mine + c, frame_of[pos]] if d == 0 else kv.at[z - d, c, pos]
        return remote(src, kv.at[z - d, c, pos], up_send, up_recv.at[c, pos, d], camtime=t_up)

    def dn_copy(c, pos, hop):
        plane = (z + hop) % PLANES
        src = kc.at[mine + c, frame_of[pos]] if hop == 0 else kv.at[plane, c, pos]
        return remote(src, kv.at[plane, c, pos], dn_send, dn_recv.at[c, pos, hop], camtime=t_dn)

    def cross_copy(c):
        return remote(kc.at[mine + c], kc.at[mine + c], c_send, c_recv, camtime=t_x)

    def part_copy(c, places):
        lo, count = places[0], len(places)
        return remote(
            x_part.at[c, pl.ds(lo, count)], x_land.at[c, pl.ds(lo, count)],
            x_part_send, x_part_recv.at[c, lo], heads=h_sib,
        )

    def project_half(c, places):
        count = len(places) * PATCH
        squares = jnp.zeros((count, DEPTH), jnp.float32)
        for pos in places:
            arrived(xg.at[pl.ds(x_slot(c, pos, 0, 0), 6 if c in TREE_X else 8)], x_recv.at[c, pos])
        for n in range(HEADS // 2):
            wide = jnp.concatenate([xg[x_slot(c, pos, n // ROW, n % ROW)] for pos in places], axis=0).astype(jnp.float32)
            squares = squares + wide * wide
            scaled[:count, n * DEPTH:(n + 1) * DEPTH] = (wide * gain_ref[n]).astype(jnp.bfloat16)
        part = jnp.dot(
            scaled[:count], w_both[...].reshape(WIDTH // 2, 6 * DEPTH), preferred_element_type=jnp.float32
        )
        for n, pos in enumerate(places):
            here = slice(n * PATCH, (n + 1) * PATCH)
            x_part[c, pos, :, :3 * DEPTH] = part[here, 3 * DEPTH:]
            x_part[c, pos, :, 3 * DEPTH:] = squares[here]
            raw_ref[c, pos] = part[here, :3 * DEPTH]
        part_copy(c, places).start()

    def project(c, places):
        lo, count = places[0], len(places)
        arrived(x_land.at[c, pl.ds(lo, count)], x_part_recv.at[c, lo])
        land = x_land[c, lo:lo + count].reshape(count * PATCH, PART)
        squares = x_part[c, lo:lo + count].reshape(count * PATCH, PART)[:, 3 * DEPTH:] + land[:, 3 * DEPTH:]
        inv_rms = lax.rsqrt(jnp.sum(squares, axis=1, keepdims=True) / WIDTH + 1e-06)
        raw = (raw_ref[c, lo:lo + count].reshape(count * PATCH, 3 * DEPTH) + land[:, :3 * DEPTH]) * inv_rms
        key = unit_rows(raw[:, DEPTH:2 * DEPTH]).astype(jnp.bfloat16)
        value = raw[:, 2 * DEPTH:]
        for n, pos in enumerate(places):
            kc[mine + c, frame_of[pos], 0] = key[n * PATCH:(n + 1) * PATCH]
            kc[mine + c, frame_of[pos], 1] = value[n * PATCH:(n + 1) * PATCH].T.astype(jnp.bfloat16)

            @pl.when(z < PLANES - 1)
            def _():
                up_copy(c, pos, 0).start()

            @pl.when(z < DOWN[c][pos])
            def _():
                dn_copy(c, pos, 0).start()

        if 1 in places:
            cross_copy(c).start()
        query = unit_rows(raw[:, :DEPTH])
        for n, pos in enumerate(places):
            qt[c, :, pos * PATCH:(pos + 1) * PATCH] = query[n * PATCH:(n + 1) * PATCH].T.astype(jnp.bfloat16)

    def bias(plane, f, c, later=True):
        return jnp.where((allowed_ref[mine + c, 2 * plane + f] == 1) & later, 0.0, MASKED).astype(jnp.float32)

    def fold(c, score, values, lanes):
        before = top_ref[c, :, lanes]
        top = jnp.maximum(before, jnp.max(score, axis=0, keepdims=True))
        expo = jnp.exp2(score - top)
        rescale = jnp.exp2(before - top)
        top_ref[c, :, lanes] = top
        total_ref[c, :, lanes] = total_ref[c, :, lanes] * rescale + jnp.sum(expo, axis=0, keepdims=True)
        acc_ref[c, :, lanes] = acc_ref[c, :, lanes] * rescale + jnp.dot(
            values, expo.astype(jnp.bfloat16), preferred_element_type=jnp.float32
        )

    def attend(c, plane):
        keys = jnp.concatenate([kv[plane, c, 0, 0], kv[plane, c, 1, 0]], axis=0)
        values = jnp.concatenate([kv[plane, c, 0, 1], kv[plane, c, 1, 1]], axis=1)
        score = jnp.dot(keys, qt[c], preferred_element_type=jnp.float32) * (sharp_ref[0, 0] * (LOG2E / DEPTH**0.5))
        score = jnp.concatenate(
            [score[:PATCH] + bias(plane, frame_of[0], c), score[PATCH:] + bias(plane, frame_of[1], c)], axis=0
        )
        fold(c, score, values, slice(0, ROWS))

    crossed = []

    def attend_cross(c):
        if not crossed:
            crossed.append(c)
            arrived(kc.at[pl.ds(theirs, GROUP)], c_recv)
        cam = mine + c
        for pos, f in enumerate(frame_of):
            lanes = slice(pos * PATCH, (pos + 1) * PATCH)
            near = [(cam, f), (adj_ref[0, cam], f), (adj_ref[1, cam], f), (cam, 0)]
            keys = jnp.concatenate([kc[n, f_, 0] for n, f_ in near], axis=0)
            values = jnp.concatenate([kc[n, f_, 1] for n, f_ in near], axis=1)
            score = jnp.dot(keys, qt[c, :, lanes], preferred_element_type=jnp.float32) * (sharp_ref[0, 0] * (LOG2E / DEPTH**0.5))
            score = jnp.concatenate(
                [score[:3 * PATCH], score[3 * PATCH:] + bias(z, 0, c, f == 1)], axis=0
            )
            fold(c, score, values, lanes)

    deliveries = {}
    for n, step in enumerate(ORDER):
        if step[0] in "UD":
            below = int(step[3]) if step[0] == "U" else PLANES - int(step[3])
            deliveries[step[1], below] = n

    def step_up(n, c, pos, d):
        @pl.when(z >= d)
        def _():
            arrived(kv.at[z - d, c, pos], up_recv.at[c, pos, d - 1])
            if d < UP[c][pos]:
                @pl.when(z < PLANES - 1)
                def _():
                    up_copy(c, pos, d).start()
            if deliveries[str(c), d] == n:
                attend(c, z - d)

    def step_dn(n, c, pos, hop):
        plane = (z + hop) % PLANES

        @pl.when(plane < DOWN[c][pos])
        def _():
            arrived(kv.at[plane, c, pos], dn_recv.at[c, pos, hop - 1])
            if hop < DOWN[c][pos]:
                dn_copy(c, pos, hop).start()
            if deliveries[str(c), PLANES - hop] == n:
                @pl.when(plane < z)
                def _():
                    attend(c, plane)

    def m_push(c):
        mixed = (acc_ref[c] / total_ref[c]).T.astype(jnp.bfloat16).reshape(2, PATCH, DEPTH)
        mstage[c] = mixed
        cam = mine + c
        slot = m_slot(cam, a, y)
        mg[slot] = mstage[c, 1]
        for chip in chips:
            a_, y_ = chip
            remote(mstage.at[c, 0], mg.at[slot], m_send, m_recv.at[c, 0], heads=head(a_, y_, p), camtime=t_x).start()
        for chip in chips:
            a_, y_ = chip
            if chip is not self_chip:
                remote(mstage.at[c, 1], mg.at[slot], m_send, m_recv.at[c, 1], heads=head(a_, y_, p)).start()

    def m_copy(c, own):
        return remote(m_part.at[c, own], m_land.at[c, own], m_part_send, m_part_recv.at[c, own], heads=h_sib)

    def project_out_half(c, own):
        arrived(xg.at[pl.ds(0, HEADS // 2 - own)], m_recv.at[c, own])
        cam = mine + c if own else theirs + c
        summed = jnp.zeros((PATCH, 2 * DEPTH), jnp.float32)
        for n in range(HEADS // 2):
            part = jnp.dot(mg[m_slot(cam, n // ROW, n % ROW)], e_both[n], preferred_element_type=jnp.float32)
            summed = summed + part.astype(jnp.bfloat16).astype(jnp.float32)
        m_part[c, own] = summed[:, DEPTH:]
        m_copy(c, own).start()
        m_own[c, own] = summed[:, :DEPTH]

    def project_out(c, own):
        arrived(m_land.at[c, own], m_part_recv.at[c, own])
        out_ref[mine + c if own else theirs + c] = (m_own[c, own] + m_land[c, own]).astype(jnp.bfloat16)

    x_push(0)
    for i in range(3):
        w_copy(i).start()
    for c in TREE_X:
        x_push(c)
    for c in range(1, GROUP):
        if c not in TREE_X:
            x_push(c)
    for load in [gain_load] + small_loads:
        load.wait()
    arrived(w_both.at[:, :, :3 * DEPTH], w_load)
    arrived(w_both.at[:, :, 3 * DEPTH:], w_recv)
    for n, step in enumerate(ORDER):
        kind, c = step[0], int(step[1:2] or 0)
        pos, hop = int(step[2:3] or 0), int(step[3:] or 0)
        if kind == "H":
            project_half(c, (pos,))
        elif kind == "P":
            project(c, (pos,))
        elif kind == "U":
            step_up(n, c, pos, hop)
        elif kind == "D":
            step_dn(n, c, pos, hop)
        elif kind == "C":
            attend_cross(c)
        elif kind == "F":
            m_push(c)
        elif kind == "X":
            if c in TREE_X:
                x_relay(c, pos)
        else:
            e_push()
    arrived(e_both, e_recv)
    for c in range(2):
        for own in range(2):
            project_out_half(c, own)
    for c in range(2):
        for own in range(2):
            project_out(c, own)
    project_out_half(2, 0)
    project_out_half(2, 1)
    project_out(2, 0)
    project_out(2, 1)

    pieces = HEADS - 1
    arrived(xg.at[pl.ds(0, GROUP * pieces)], x_send)
    arrived(xg.at[pl.ds(0, GROUP * pieces)], m_send)
    arrived(xg.at[pl.ds(0, HEADS - 2)], e_send)
    arrived(xg.at[pl.ds(0, 3 * HEADS // 2)], w_send)
    arrived(x_part, x_part_send)
    arrived(m_part, m_part_send)
    arrived(kc.at[pl.ds(mine, GROUP)], c_send)
    for plane in range(PLANES):
        frames = [(c, pos) for c in range(GROUP) for pos in range(2)]
        ups = sum(min(UP[c][pos], plane + 1) for c, pos in frames) if plane < PLANES - 1 else 0
        downs = sum((plane + hop) % PLANES < DOWN[c][pos] for c, pos in frames for hop in range(DOWN[c][pos]))

        @pl.when(z == plane)
        def _():
            if ups:
                arrived(xg.at[pl.ds(0, 2 * ups)], up_send)
            if downs:
                arrived(xg.at[pl.ds(0, 2 * downs)], dn_send)


def on_device(
    hidden_patch_vectors,
    entry_rms_multiplier,
    lookup_projection_matrix,
    exit_projection_matrix,
    probe_sharpness,
    adjacent_camera_pairs,
    prior_frame_allowed,
):
    frames, cams, patches, local_width = hidden_patch_vectors.shape
    hbm = pl.BlockSpec(memory_space=pltpu.HBM)
    dma = pltpu.SemaphoreType.DMA
    bf16, f32 = jnp.bfloat16, jnp.float32
    result = pl.pallas_call(
        kernel,
        out_shape=jax.ShapeDtypeStruct((cams, patches, local_width), bf16),
        in_specs=[hbm] * 7,
        out_specs=pl.BlockSpec(memory_space=pltpu.VMEM),
        scratch_shapes=[
            pltpu.VMEM((GROUP * HEADS, PATCH, DEPTH), bf16),
            pltpu.VMEM((GROUP * HEADS, PATCH, DEPTH), bf16),
            pltpu.VMEM((GROUP, 2, PATCH, DEPTH), bf16),
            pltpu.VMEM((PLANES, GROUP, 2, 2, PATCH, DEPTH), bf16),
            pltpu.VMEM((2 * GROUP, 2, 2, PATCH, DEPTH), bf16),
            pltpu.VMEM((HEADS // 2, 1, DEPTH), f32),
            pltpu.VMEM((HEADS // 2, DEPTH, 6 * DEPTH), bf16),
            pltpu.VMEM((HEADS // 2, DEPTH, 2 * DEPTH), bf16),
            pltpu.VMEM((ROWS, WIDTH // 2), bf16),
            pltpu.VMEM((GROUP, 2, PATCH, PART), f32),
            pltpu.VMEM((GROUP, 2, PATCH, PART), f32),
            pltpu.VMEM((GROUP, 2, PATCH, DEPTH), f32),
            pltpu.VMEM((GROUP, 2, PATCH, DEPTH), f32),
            pltpu.VMEM((GROUP, 2, PATCH, DEPTH), f32),
            pltpu.VMEM((GROUP, 2, PATCH, 3 * DEPTH), f32),
            pltpu.VMEM((GROUP, DEPTH, ROWS), bf16),
            pltpu.VMEM((GROUP, 1, ROWS), f32),
            pltpu.VMEM((GROUP, 1, ROWS), f32),
            pltpu.VMEM((GROUP, DEPTH, ROWS), f32),
            pltpu.SMEM((1, 1), f32),
            pltpu.SMEM((2, cams), jnp.int32),
            pltpu.SMEM((cams, PLANES * 2), jnp.int32),
            dma((GROUP, 2)),
            dma((GROUP, 2)),
            dma((GROUP, 2)),
            dma((GROUP, 2)),
            dma((GROUP, 2)),
            dma((GROUP, 2, 4)),
            dma((GROUP, 2, 4)),
            dma((SINGLE_SEMS,)),
        ],
        compiler_params=pltpu.CompilerParams(
            collective_id=0, has_side_effects=True, vmem_limit_bytes=48 * 1024 * 1024
        ),
    )(*[operand if operand.size == 1 else pltpu.with_memory_space_constraint(operand, pltpu.HBM) for operand in (
        hidden_patch_vectors.reshape(cams, patches, local_width),
        entry_rms_multiplier.reshape(HEADS // 2, 2, 1, DEPTH),
        lookup_projection_matrix.transpose(1, 0, 2).reshape(3, HEADS // 2, 2, DEPTH, DEPTH),
        exit_projection_matrix,
        probe_sharpness.reshape(1, 1),
        adjacent_camera_pairs.T,
        prior_frame_allowed.T,
    )])
    return result.reshape(frames, cams, patches, local_width)


def solution(mesh):
    placed = (
        P("camtime", None, None, "heads"),
        P(),
        P(None, None, "heads"),
        P("heads", None),
        P("heads"),
        P(),
        P(),
    )
    return jax.shard_map(
        on_device,
        mesh=mesh,
        in_specs=placed,
        out_specs=P("camtime", None, None, "heads"),
        check_vma=False,
    )
```

```python
import jax
import jax.numpy as jnp
from jax import lax
from jax.experimental import pallas as pl
from jax.experimental.pallas import tpu as pltpu
from jax.sharding import PartitionSpec as P

HEADS = 16
ROW = 4
PLANES = 8
GROUP = 3
DEPTH = 128
PATCH = 128
WIDTH = HEADS * DEPTH
ROWS = 2 * PATCH
MASKED = -3e38
LOWEST = -1e30
LOG2E = 1.4426950408889634
SINGLE_SEMS = 18
PART = 4 * DEPTH
UP = ((3, 4), (3, 3), (4, 4))
DOWN = ((4, 3), (4, 4), (3, 3))
TREE_X = (2,)
ORDER = (
    "H00", "P00", "H01", "P01", "X20", "H10", "X21", "U001", "D001", "P10", "H11", "U011",
    "D011", "P11", "H20", "U101", "U002", "D002", "D101", "U012", "P20", "H21",
    "D012", "U003", "D111", "D003", "P21", "E", "D102", "U013", "D013",
    "U111", "U201", "D112", "D201", "D004", "C0", "U102", "U014", "F0",
    "C1", "U211", "C2", "U112", "D103", "D113", "D211", "U202", "U103", "D104", "U212", "D202",
    "U113", "D114", "F1", "U203", "D212", "U213", "D203", "U204", "D213", "U214",
    "F2",
)


def unit_rows(raw):
    return raw * lax.rsqrt(jnp.mean(raw * raw, axis=-1, keepdims=True) + 1e-06)


def kernel(
    x_hbm, gain_hbm, w_hbm, e_hbm, sharp_hbm, adj_hbm, allowed_hbm, out_ref,
    xg, mg, mstage, kv, kc, gain_ref, w_both, e_both, scaled, x_part, x_land, m_part, m_land, m_own,
    raw_ref, qt, top_ref, total_ref, acc_ref, x_ref, sharp_ref, adj_ref, allowed_ref,
    x_recv, x_row, x_part_recv, m_recv, m_part_recv, up_recv, dn_recv, sems,
):
    (x_send, x_part_send, m_send, m_part_send, up_send, dn_send, c_recv, c_send,
     e_recv, e_send, w_load, w_recv, w_send, gain_sem, sharp_sem, adj_sem, allowed_sem, x_sem) = [sems.at[n] for n in range(SINGLE_SEMS)]
    t = lax.axis_index("camtime")
    h = lax.axis_index("heads")
    z, j = t // 2, t % 2
    a, y, p = h // 8, (h // 2) % ROW, h % 2

    def head(a_, y_, p_):
        return a_ * 8 + y_ * 2 + p_

    rows = [y, (y + 1) % ROW, (y + 3) % ROW, (y + 2) % ROW]
    h_sib = head(a, y, 1 - p)
    t_x = z * 2 + 1 - j
    t_up = ((z + 1) % PLANES) * 2 + j
    t_dn = ((z + PLANES - 1) % PLANES) * 2 + j
    mine = GROUP * j
    theirs = GROUP * (1 - j)

    def remote(src, dst, send, recv, heads=None, camtime=None):
        return pltpu.make_async_remote_copy(
            src_ref=src, dst_ref=dst, send_sem=send, recv_sem=recv,
            device_id={"camtime": t if camtime is None else camtime, "heads": h if heads is None else heads},
            device_id_type=pl.DeviceIdType.MESH,
        )

    def arrived(ref, sem):
        pltpu.make_async_copy(ref, ref, sem).wait()

    barrier = pltpu.get_barrier_semaphore()

    def greet(camtime, heads):
        pl.semaphore_signal(
            barrier, inc=1, device_id={"camtime": camtime, "heads": heads}, device_id_type=pl.DeviceIdType.MESH
        )

    for other in range(2, HEADS, 2):
        greet(t, (h + other) % HEADS)
    for other in range(0, HEADS, 2):
        greet(t_x, (h + other) % HEADS)
    greet(t, h_sib)
    greet(t_up, h)
    greet(t_dn, h)

    frame_of = (1 - j, j)

    def x_slot(c, pos, a_, y_):
        return ((c * 2 + pos) * ROW + y_) * 2 + a_

    def m_slot(cam, a_, y_):
        return (cam * ROW + y_) * 2 + a_

    x_load = pltpu.make_async_copy(x_hbm, x_ref, x_sem)
    x_load.start()
    for c in range(GROUP):
        pltpu.make_async_copy(x_hbm.at[mine + c], xg.at[x_slot(c, 1, a, y)], (x_row if c in TREE_X else x_recv).at[c, 1]).start()
    gain_load = pltpu.make_async_copy(gain_hbm.at[:, p], gain_ref, gain_sem)
    gain_load.start()
    small_loads = [
        pltpu.make_async_copy(sharp_hbm, sharp_ref, sharp_sem),
        pltpu.make_async_copy(adj_hbm, adj_ref, adj_sem),
        pltpu.make_async_copy(allowed_hbm, allowed_ref, allowed_sem),
    ]
    for load in small_loads:
        load.start()
    for i in range(3):
        pltpu.make_async_copy(w_hbm.at[i, :, p], w_both.at[:, :, i * DEPTH:(i + 1) * DEPTH], w_load).start()
    for c in range(GROUP):
        top_ref[c] = jnp.full((1, ROWS), LOWEST, jnp.float32)
        total_ref[c] = jnp.zeros((1, ROWS), jnp.float32)
        acc_ref[c] = jnp.zeros((DEPTH, ROWS), jnp.float32)
    pl.semaphore_wait(barrier, HEADS + 2)
    x_load.wait()

    near = [(a_, y_) for y_ in rows for a_ in (1 - a, a)]
    self_chip = near[1]
    chips = near[6:8] + near[2:6] + near[0:2]

    def row_push(buf, slot, send, recv):
        for y_ in rows[:0:-1]:
            remote(buf.at[pl.ds(slot, 2)], buf.at[pl.ds(slot, 2)], send, recv, heads=head(a, y_, p)).start()

    def x_push(c):
        if c in TREE_X:
            for a_ in (1 - a, a):
                remote(x_ref.at[theirs + c], xg.at[x_slot(c, 0, a, y)], x_send, x_row.at[c, 0],
                       heads=head(a_, y, p), camtime=t_x).start()
            remote(x_ref.at[mine + c], xg.at[x_slot(c, 1, a, y)], x_send, x_row.at[c, 1],
                   heads=head(1 - a, y, p)).start()
            return
        for chip in chips:
            a_, y_ = chip
            remote(x_ref.at[theirs + c], xg.at[x_slot(c, 0, a, y)], x_send, x_recv.at[c, 0],
                   heads=head(a_, y_, p), camtime=t_x).start()
        for chip in chips:
            a_, y_ = chip
            if chip is not self_chip:
                remote(x_ref.at[mine + c], xg.at[x_slot(c, 1, a, y)], x_send, x_recv.at[c, 1],
                       heads=head(a_, y_, p)).start()

    def x_relay(c, pos):
        slot = x_slot(c, pos, 0, y)
        arrived(xg.at[pl.ds(slot, 2)], x_row.at[c, pos])
        row_push(xg, slot, x_send, x_recv.at[c, pos])

    def w_copy(i):
        return remote(
            w_hbm.at[i, :, 1 - p], w_both.at[:, :, (3 + i) * DEPTH:(4 + i) * DEPTH], w_send, w_recv, heads=h_sib
        )

    def e_push():
        for chip in chips:
            a_, y_ = chip
            for side, p_ in enumerate((p, 1 - p)):
                src = e_hbm.at[:, pl.ds(pl.multiple_of(head(a_, y_, p_) * DEPTH, DEPTH), DEPTH)]
                dst = e_both.at[a * ROW + y, :, side * DEPTH:(side + 1) * DEPTH]
                if chip is self_chip:
                    pltpu.make_async_copy(src, dst, e_recv).start()
                else:
                    remote(src, dst, e_send, e_recv, heads=head(a_, y_, p)).start()


    def up_copy(c, pos, d):
        src = kc.at[mine + c, frame_of[pos]] if d == 0 else kv.at[z - d, c, pos]
        return remote(src, kv.at[z - d, c, pos], up_send, up_recv.at[c, pos, d], camtime=t_up)

    def dn_copy(c, pos, hop):
        plane = (z + hop) % PLANES
        src = kc.at[mine + c, frame_of[pos]] if hop == 0 else kv.at[plane, c, pos]
        return remote(src, kv.at[plane, c, pos], dn_send, dn_recv.at[c, pos, hop], camtime=t_dn)

    def cross_copy(c):
        return remote(kc.at[mine + c], kc.at[mine + c], c_send, c_recv, camtime=t_x)

    def part_copy(c, places):
        lo, count = places[0], len(places)
        return remote(
            x_part.at[c, pl.ds(lo, count)], x_land.at[c, pl.ds(lo, count)],
            x_part_send, x_part_recv.at[c, lo], heads=h_sib,
        )

    def project_half(c, places):
        count = len(places) * PATCH
        squares = jnp.zeros((count, DEPTH), jnp.float32)
        for pos in places:
            arrived(xg.at[pl.ds(x_slot(c, pos, 0, 0), 6 if c in TREE_X else 8)], x_recv.at[c, pos])
        for n in range(HEADS // 2):
            wide = jnp.concatenate([xg[x_slot(c, pos, n // ROW, n % ROW)] for pos in places], axis=0).astype(jnp.float32)
            squares = squares + wide * wide
            scaled[:count, n * DEPTH:(n + 1) * DEPTH] = (wide * gain_ref[n]).astype(jnp.bfloat16)
        part = jnp.dot(
            scaled[:count], w_both[...].reshape(WIDTH // 2, 6 * DEPTH), preferred_element_type=jnp.float32
        )
        for n, pos in enumerate(places):
            here = slice(n * PATCH, (n + 1) * PATCH)
            x_part[c, pos, :, :3 * DEPTH] = part[here, 3 * DEPTH:]
            x_part[c, pos, :, 3 * DEPTH:] = squares[here]
            raw_ref[c, pos] = part[here, :3 * DEPTH]
        part_copy(c, places).start()

    def project(c, places):
        lo, count = places[0], len(places)
        arrived(x_land.at[c, pl.ds(lo, count)], x_part_recv.at[c, lo])
        land = x_land[c, lo:lo + count].reshape(count * PATCH, PART)
        squares = x_part[c, lo:lo + count].reshape(count * PATCH, PART)[:, 3 * DEPTH:] + land[:, 3 * DEPTH:]
        inv_rms = lax.rsqrt(jnp.sum(squares, axis=1, keepdims=True) / WIDTH + 1e-06)
        raw = (raw_ref[c, lo:lo + count].reshape(count * PATCH, 3 * DEPTH) + land[:, :3 * DEPTH]) * inv_rms
        key = unit_rows(raw[:, DEPTH:2 * DEPTH]).astype(jnp.bfloat16)
        value = raw[:, 2 * DEPTH:]
        for n, pos in enumerate(places):
            kc[mine + c, frame_of[pos], 0] = key[n * PATCH:(n + 1) * PATCH]
            kc[mine + c, frame_of[pos], 1] = value[n * PATCH:(n + 1) * PATCH].T.astype(jnp.bfloat16)

            @pl.when(z < PLANES - 1)
            def _():
                up_copy(c, pos, 0).start()

            @pl.when(z < DOWN[c][pos])
            def _():
                dn_copy(c, pos, 0).start()

        if 1 in places:
            cross_copy(c).start()
        query = unit_rows(raw[:, :DEPTH])
        for n, pos in enumerate(places):
            qt[c, :, pos * PATCH:(pos + 1) * PATCH] = query[n * PATCH:(n + 1) * PATCH].T.astype(jnp.bfloat16)

    def bias(plane, f, c, later=True):
        return jnp.where((allowed_ref[mine + c, 2 * plane + f] == 1) & later, 0.0, MASKED).astype(jnp.float32)

    def fold(c, score, values, lanes):
        before = top_ref[c, :, lanes]
        top = jnp.maximum(before, jnp.max(score, axis=0, keepdims=True))
        expo = jnp.exp2(score - top)
        rescale = jnp.exp2(before - top)
        top_ref[c, :, lanes] = top
        total_ref[c, :, lanes] = total_ref[c, :, lanes] * rescale + jnp.sum(expo, axis=0, keepdims=True)
        acc_ref[c, :, lanes] = acc_ref[c, :, lanes] * rescale + jnp.dot(
            values, expo.astype(jnp.bfloat16), preferred_element_type=jnp.float32
        )

    def attend(c, plane):
        keys = jnp.concatenate([kv[plane, c, 0, 0], kv[plane, c, 1, 0]], axis=0)
        values = jnp.concatenate([kv[plane, c, 0, 1], kv[plane, c, 1, 1]], axis=1)
        score = jnp.dot(keys, qt[c], preferred_element_type=jnp.float32) * (sharp_ref[0, 0] * (LOG2E / DEPTH**0.5))
        score = jnp.concatenate(
            [score[:PATCH] + bias(plane, frame_of[0], c), score[PATCH:] + bias(plane, frame_of[1], c)], axis=0
        )
        fold(c, score, values, slice(0, ROWS))

    crossed = []

    def attend_cross(c):
        if not crossed:
            crossed.append(c)
            arrived(kc.at[pl.ds(theirs, GROUP)], c_recv)
        cam = mine + c
        for pos, f in enumerate(frame_of):
            lanes = slice(pos * PATCH, (pos + 1) * PATCH)
            near = [(cam, f), (adj_ref[0, cam], f), (adj_ref[1, cam], f), (cam, 0)]
            keys = jnp.concatenate([kc[n, f_, 0] for n, f_ in near], axis=0)
            values = jnp.concatenate([kc[n, f_, 1] for n, f_ in near], axis=1)
            score = jnp.dot(keys, qt[c, :, lanes], preferred_element_type=jnp.float32) * (sharp_ref[0, 0] * (LOG2E / DEPTH**0.5))
            score = jnp.concatenate(
                [score[:3 * PATCH], score[3 * PATCH:] + bias(z, 0, c, f == 1)], axis=0
            )
            fold(c, score, values, lanes)

    deliveries = {}
    for n, step in enumerate(ORDER):
        if step[0] in "UD":
            below = int(step[3]) if step[0] == "U" else PLANES - int(step[3])
            deliveries[step[1], below] = n

    def step_up(n, c, pos, d):
        @pl.when(z >= d)
        def _():
            arrived(kv.at[z - d, c, pos], up_recv.at[c, pos, d - 1])
            if d < UP[c][pos]:
                @pl.when(z < PLANES - 1)
                def _():
                    up_copy(c, pos, d).start()
            if deliveries[str(c), d] == n:
                attend(c, z - d)

    def step_dn(n, c, pos, hop):
        plane = (z + hop) % PLANES

        @pl.when(plane < DOWN[c][pos])
        def _():
            arrived(kv.at[plane, c, pos], dn_recv.at[c, pos, hop - 1])
            if hop < DOWN[c][pos]:
                dn_copy(c, pos, hop).start()
            if deliveries[str(c), PLANES - hop] == n:
                @pl.when(plane < z)
                def _():
                    attend(c, plane)

    def m_push(c):
        mixed = (acc_ref[c] / total_ref[c]).T.astype(jnp.bfloat16).reshape(2, PATCH, DEPTH)
        mstage[c] = mixed
        cam = mine + c
        slot = m_slot(cam, a, y)
        mg[slot] = mstage[c, 1]
        for chip in chips:
            to = head(chip[0], chip[1], p)
            remote(mstage.at[c, 0], mg.at[slot], m_send, m_recv.at[c, 0], heads=to, camtime=t_x).start()
            if chip is not self_chip:
                remote(mstage.at[c, 1], mg.at[slot], m_send, m_recv.at[c, 1], heads=to).start()

    def m_copy(c, own):
        return remote(m_part.at[c, own], m_land.at[c, own], m_part_send, m_part_recv.at[c, own], heads=h_sib)

    def project_out_half(c, own):
        arrived(xg.at[pl.ds(0, HEADS // 2 - own)], m_recv.at[c, own])
        cam = mine + c if own else theirs + c
        summed = jnp.zeros((PATCH, 2 * DEPTH), jnp.float32)
        for n in range(HEADS // 2):
            part = jnp.dot(mg[m_slot(cam, n // ROW, n % ROW)], e_both[n], preferred_element_type=jnp.float32)
            summed = summed + part.astype(jnp.bfloat16).astype(jnp.float32)
        m_part[c, own] = summed[:, DEPTH:]
        m_copy(c, own).start()
        m_own[c, own] = summed[:, :DEPTH]

    def project_out(c, own):
        arrived(m_land.at[c, own], m_part_recv.at[c, own])
        out_ref[mine + c if own else theirs + c] = (m_own[c, own] + m_land[c, own]).astype(jnp.bfloat16)

    x_push(0)
    for i in range(3):
        w_copy(i).start()
    for c in TREE_X:
        x_push(c)
    for c in range(1, GROUP):
        if c not in TREE_X:
            x_push(c)
    for load in [gain_load] + small_loads:
        load.wait()
    arrived(w_both.at[:, :, :3 * DEPTH], w_load)
    arrived(w_both.at[:, :, 3 * DEPTH:], w_recv)
    for n, step in enumerate(ORDER):
        kind, c = step[0], int(step[1:2] or 0)
        pos, hop = int(step[2:3] or 0), int(step[3:] or 0)
        if kind == "H":
            project_half(c, (pos,))
        elif kind == "P":
            project(c, (pos,))
        elif kind == "U":
            step_up(n, c, pos, hop)
        elif kind == "D":
            step_dn(n, c, pos, hop)
        elif kind == "C":
            attend_cross(c)
        elif kind == "F":
            m_push(c)
        elif kind == "X":
            if c in TREE_X:
                x_relay(c, pos)
        else:
            e_push()
    arrived(e_both, e_recv)
    for c in range(2):
        for own in range(2):
            project_out_half(c, own)
    for c in range(2):
        for own in range(2):
            project_out(c, own)
    project_out_half(2, 0)
    project_out_half(2, 1)
    project_out(2, 0)
    project_out(2, 1)

    pieces = HEADS - 1
    arrived(xg.at[pl.ds(0, GROUP * pieces)], x_send)
    arrived(xg.at[pl.ds(0, GROUP * pieces)], m_send)
    arrived(xg.at[pl.ds(0, HEADS - 2)], e_send)
    arrived(xg.at[pl.ds(0, 3 * HEADS // 2)], w_send)
    arrived(x_part, x_part_send)
    arrived(m_part, m_part_send)
    arrived(kc.at[pl.ds(mine, GROUP)], c_send)
    for plane in range(PLANES):
        frames = [(c, pos) for c in range(GROUP) for pos in range(2)]
        ups = sum(min(UP[c][pos], plane + 1) for c, pos in frames) if plane < PLANES - 1 else 0
        downs = sum((plane + hop) % PLANES < DOWN[c][pos] for c, pos in frames for hop in range(DOWN[c][pos]))

        @pl.when(z == plane)
        def _():
            if ups:
                arrived(xg.at[pl.ds(0, 2 * ups)], up_send)
            if downs:
                arrived(xg.at[pl.ds(0, 2 * downs)], dn_send)


def on_device(
    hidden_patch_vectors,
    entry_rms_multiplier,
    lookup_projection_matrix,
    exit_projection_matrix,
    probe_sharpness,
    adjacent_camera_pairs,
    prior_frame_allowed,
):
    frames, cams, patches, local_width = hidden_patch_vectors.shape
    hbm = pl.BlockSpec(memory_space=pltpu.HBM)
    dma = pltpu.SemaphoreType.DMA
    bf16, f32 = jnp.bfloat16, jnp.float32
    result = pl.pallas_call(
        kernel,
        out_shape=jax.ShapeDtypeStruct((cams, patches, local_width), bf16),
        in_specs=[hbm] * 7,
        out_specs=pl.BlockSpec(memory_space=pltpu.VMEM),
        scratch_shapes=[
            pltpu.VMEM((GROUP * HEADS, PATCH, DEPTH), bf16),
            pltpu.VMEM((GROUP * HEADS, PATCH, DEPTH), bf16),
            pltpu.VMEM((GROUP, 2, PATCH, DEPTH), bf16),
            pltpu.VMEM((PLANES, GROUP, 2, 2, PATCH, DEPTH), bf16),
            pltpu.VMEM((2 * GROUP, 2, 2, PATCH, DEPTH), bf16),
            pltpu.VMEM((HEADS // 2, 1, DEPTH), f32),
            pltpu.VMEM((HEADS // 2, DEPTH, 6 * DEPTH), bf16),
            pltpu.VMEM((HEADS // 2, DEPTH, 2 * DEPTH), bf16),
            pltpu.VMEM((ROWS, WIDTH // 2), bf16),
            pltpu.VMEM((GROUP, 2, PATCH, PART), f32),
            pltpu.VMEM((GROUP, 2, PATCH, PART), f32),
            pltpu.VMEM((GROUP, 2, PATCH, DEPTH), f32),
            pltpu.VMEM((GROUP, 2, PATCH, DEPTH), f32),
            pltpu.VMEM((GROUP, 2, PATCH, DEPTH), f32),
            pltpu.VMEM((GROUP, 2, PATCH, 3 * DEPTH), f32),
            pltpu.VMEM((GROUP, DEPTH, ROWS), bf16),
            pltpu.VMEM((GROUP, 1, ROWS), f32),
            pltpu.VMEM((GROUP, 1, ROWS), f32),
            pltpu.VMEM((GROUP, DEPTH, ROWS), f32),
            pltpu.VMEM((cams, patches, local_width), bf16),
            pltpu.SMEM((1, 1), f32),
            pltpu.SMEM((2, cams), jnp.int32),
            pltpu.SMEM((cams, PLANES * 2), jnp.int32),
            dma((GROUP, 2)),
            dma((GROUP, 2)),
            dma((GROUP, 2)),
            dma((GROUP, 2)),
            dma((GROUP, 2)),
            dma((GROUP, 2, 4)),
            dma((GROUP, 2, 4)),
            dma((SINGLE_SEMS,)),
        ],
        compiler_params=pltpu.CompilerParams(
            collective_id=0, has_side_effects=True, vmem_limit_bytes=48 * 1024 * 1024
        ),
    )(*[operand if operand.size == 1 else pltpu.with_memory_space_constraint(operand, pltpu.HBM) for operand in (
        hidden_patch_vectors.reshape(cams, patches, local_width),
        entry_rms_multiplier.reshape(HEADS // 2, 2, 1, DEPTH),
        lookup_projection_matrix.transpose(1, 0, 2).reshape(3, HEADS // 2, 2, DEPTH, DEPTH),
        exit_projection_matrix,
        probe_sharpness.reshape(1, 1),
        adjacent_camera_pairs.T,
        prior_frame_allowed.T,
    )])
    return result.reshape(frames, cams, patches, local_width)


def solution(mesh):
    placed = (
        P("camtime", None, None, "heads"),
        P(),
        P(None, None, "heads"),
        P("heads", None),
        P("heads"),
        P(),
        P(),
    )
    return jax.shard_map(
        on_device,
        mesh=mesh,
        in_specs=placed,
        out_specs=P("camtime", None, None, "heads"),
        check_vma=False,
    )
```
